512 devices in a mesh: dp: 64 (over x, z, core), tensor: 8 (over y).
Axes of the slice: x: 4, y: 8, z: 8, core: 2. Of those that a mesh axis runs over, the one named last changes fastest.
Arguments:
- queries: bfloat16 [3072, 10240], P('dp', 'tensor'), may hold values from -24 to 24
- new_kv: bfloat16 [3072, 2, 10240], P('dp', None, 'tensor'), may hold values from -6 to 6
- prefix_kv: bfloat16 [128, 2, 10240], P(None, None, 'tensor'), may hold values from -20 to 20
- suffix_kv: bfloat16 [3072, 8, 2, 10240], P('dp', None, None, 'tensor'), may hold values from -20 to 20
- suffix_len: int32 [3072], replicated, may hold values from 1 to 8, as said below
- parents: int32 [3072], replicated, may hold values from 0 to 3071, as said below
- out_weight: bfloat16 [10240, 10240], P('tensor', 'dp'), may hold values from -1 to 1
- residual: bfloat16 [3072, 10240], P('tensor', 'dp'), may hold values from -1.796875 to 1.796875
- steer_dict: bfloat16 [1024, 10240], P(None, 'dp'), may hold values from -1.796875 to 1.796875
- steer_ids: int32 [3072, 4], P('tensor'), may hold values from 0 to 1023
- steer_strength: float32 [3072, 4], P('tensor'), may hold values from 0.5 to 2
- norm_gain: float32 [10240], P('dp'), may hold values from 0.5 to 1.5
- norm_bias: float32 [10240], P('dp'), may hold values from -3 to 3
Outputs:
- mixed: bfloat16 [3072, 10240], P('tensor', 'dp')
The draws below stay inside these ranges and needn't reach their ends.
Inputs may be any that keep to these rules, and one draw needn't show every extreme that they name: Of the 48 beams of one aligned block, at most 2 have parents in any one aligned block, and in every block some source block holds exactly 2 of them. `suffix_len`: every aligned block of 48 beams has one of length 8.
All inputs are finite; a program needn't handle non-finite values.
Results may differ from the reference program's by a relative error of at most 0.0051.
Values may be sent and summed in bfloat16 or wider, within the bound.
A program may use at most 64 MiB of HBM per device.

```python
import math
import jax
import jax.numpy as jnp
from jax import lax

D = 10240
HEADS = 80
HEAD = 128
B_DEV = 48
S_SUF = 8
P_PRE = 128
FEATS = 1024
K_STEER = 4
CAP = 2
BEAMS = 3072


def draw_parents(key, part):
    key = jax.random.fold_in(key, 11)
    groups = BEAMS // B_DEV

    def one_group(group_key):
        key_list = jax.random.split(group_key, 4)
        source_order = jax.random.permutation(key_list[0], groups)
        source_pool = jnp.repeat(source_order, CAP)
        rest_slots = jax.random.permutation(key_list[1], CAP * groups - CAP)[:B_DEV - CAP] + CAP
        chosen = jnp.concatenate([jnp.arange(CAP, dtype=jnp.int32), rest_slots.astype(jnp.int32)])
        sources = source_pool[chosen]
        sources = sources[jax.random.permutation(key_list[2], B_DEV)]
        local_index = jax.random.randint(key_list[3], (B_DEV,), 0, B_DEV)
        return (sources * B_DEV + local_index).astype(jnp.int32)
    group_keys = jax.random.split(key, groups)
    return jax.vmap(one_group)(group_keys).reshape(BEAMS)


def draw_suffix_len(key, part):
    key = jax.random.fold_in(key, 12)
    first_key, second_key = jax.random.split(key)
    length_table = jax.random.randint(first_key, (BEAMS // B_DEV, B_DEV), 1, S_SUF + 1)
    top_slot = jax.random.randint(second_key, (BEAMS // B_DEV, 1), 0, B_DEV)
    length_table = jnp.where(jnp.arange(B_DEV)[None, :] == top_slot, S_SUF, length_table)
    return length_table.reshape(BEAMS).astype(jnp.int32)


def draw_queries(key, part):
    key = jax.random.fold_in(key, 13)
    first_key = jax.random.fold_in(key, 0)
    return jnp.clip(jax.random.normal(first_key, (BEAMS, D), jnp.float32), -6.0, 6.0).astype(jnp.bfloat16)


def draw_prefix_kv(key, part):
    key = jax.random.fold_in(key, 14)
    first_key = jax.random.fold_in(key, 0)
    return jnp.clip(jax.random.normal(first_key, (P_PRE, 2, D), jnp.float32), -6.0, 6.0).astype(jnp.bfloat16)


def draw_suffix_kv(key, part):
    key = jax.random.fold_in(key, 15)
    first_key = jax.random.fold_in(key, 0)
    return jnp.clip(jax.random.normal(first_key, (BEAMS, S_SUF, 2, D), jnp.float32), -6.0, 6.0).astype(jnp.bfloat16)


def plant(values, own_key, low, top_value):
    longest = values.shape.index(max(values.shape))
    spots = []
    for shift in (0, 1):
        where = [jax.random.randint(jax.random.fold_in(own_key, axis), (), 0, length) for axis, length in enumerate(values.shape)]
        where[longest] = (where[longest] + shift) % values.shape[longest]
        spots.append(tuple(where))
    return values.at[spots[0]].set(low).at[spots[1]].set(top_value)


def shard_levels(own_key, extent, shards, least, largest):
    gain = 1.0
    for axis_at, parts in shards:
        heights = jax.random.uniform(jax.random.fold_in(jax.random.fold_in(own_key, 6), axis_at), (parts,), jnp.float32, least / len(shards), largest / len(shards))
        gain = gain * jnp.repeat(jnp.exp(heights), extent[axis_at] // parts).reshape((-1,) + (1,) * (len(extent) - 1 - axis_at))
    return gain


def gaussian(key, extent, width, most, shards=(), kind=jnp.bfloat16):
    gain = shard_levels(key, extent, shards, -0.22, 0.18) if shards else 1.0
    result = jax.random.normal(key, extent, jnp.float32) * width * gain
    return jnp.minimum(jnp.maximum(result, -most), most).astype(kind)


def setup_inputs(seed: int = 0) -> dict:
    keys = jax.random.split(jax.random.key(seed), 14)
    queries = draw_queries(jax.random.fold_in(keys[13], 71), 0)
    new_kv = gaussian(keys[1], (BEAMS, 2, D), 1.0, 6.0, ((0, 64), (2, 8)))
    prefix_kv = draw_prefix_kv(jax.random.fold_in(keys[13], 71), 0)
    suffix_kv = draw_suffix_kv(jax.random.fold_in(keys[13], 71), 0)
    suffix_len = draw_suffix_len(jax.random.fold_in(keys[13], 71), 0)
    parents = draw_parents(jax.random.fold_in(keys[13], 71), 0)
    out_weight = gaussian(keys[6], (D, D), (max(1, D // 256)) ** -0.5, 1.0, ((0, 8), (1, 64)))
    residual = gaussian(keys[7], (BEAMS, D), 0.3, 1.796875, ((0, 8), (1, 64)))
    steer_dict = gaussian(keys[8], (FEATS, D), 0.3, 1.796875, ((1, 64),))
    steer_ids = plant(jax.random.randint(keys[9], (BEAMS, K_STEER), 0, FEATS), jax.random.fold_in(keys[9], 1), 0, FEATS - 1).astype(jnp.int32)
    steer_strength = jnp.clip(0.5 + 1.5 * jax.random.uniform(keys[10], (BEAMS, K_STEER), jnp.float32) ** shard_levels(keys[10], (BEAMS, K_STEER), ((0, 8),), -0.2, 0.2), 0.5, 2.0)
    norm_gain = jnp.clip(1.0 + 0.1 * jax.random.normal(keys[11], (D,), jnp.float32), 0.5, 1.5)
    norm_bias = gaussian(keys[12], (D,), 0.5, 3.0, ((0, 64),), jnp.float32)
    return {"queries": queries, "new_kv": new_kv, "prefix_kv": prefix_kv, "suffix_kv": suffix_kv, "suffix_len": suffix_len, "parents": parents, "out_weight": out_weight, "residual": residual, "steer_dict": steer_dict, "steer_ids": steer_ids, "steer_strength": steer_strength, "norm_gain": norm_gain, "norm_bias": norm_bias}


neg_fill = -1e+30

def live_weights(scores, live_len):
    span_len = scores.shape[-1]
    usable = jnp.arange(span_len)[None, None, :] < live_len[:, None, None]
    masked = jnp.where(usable, scores, neg_fill)
    peak_score = lax.optimization_barrier(jnp.max(masked, axis=-1))
    expo_vals = jnp.where(usable, jnp.exp(masked - peak_score[..., None]), 0.0)
    return (peak_score, lax.optimization_barrier(jnp.sum(expo_vals, axis=-1)), expo_vals.astype(jnp.bfloat16))

def prefix_part(query_rows, key_rows, value_rows, score_scale):
    scores = jnp.einsum('nhe,the->nht', query_rows.astype(jnp.float32), key_rows.astype(jnp.float32)) * score_scale
    peak_score = lax.optimization_barrier(jnp.max(scores, axis=-1))
    expo_vals = jnp.exp(scores - peak_score[..., None])
    weights = expo_vals.astype(jnp.bfloat16)
    partial_out = jnp.einsum('nht,the->nhe', weights.astype(jnp.float32), value_rows.astype(jnp.float32))
    return (peak_score, lax.optimization_barrier(jnp.sum(expo_vals, axis=-1)), partial_out)

def suffix_part(query_rows, key_rows, value_rows, live_len, score_scale):
    scores = jnp.einsum('nhe,nthe->nht', query_rows.astype(jnp.float32), key_rows.astype(jnp.float32)) * score_scale
    peak_score, weight_sum, weights = live_weights(scores, live_len)
    partial_out = jnp.einsum('nht,nthe->nhe', weights.astype(jnp.float32), value_rows.astype(jnp.float32))
    return (peak_score, weight_sum, partial_out)

def combine(prefix_parts, suffix_parts, self_score, self_value):
    peak_score = jnp.maximum(jnp.maximum(prefix_parts[0], suffix_parts[0]), self_score)
    lift_prefix = jnp.exp(prefix_parts[0] - peak_score)
    lift_suffix = jnp.exp(suffix_parts[0] - peak_score)
    lift_self = jnp.exp(self_score - peak_score)
    numerator = lift_prefix[..., None] * prefix_parts[2] + lift_suffix[..., None] * suffix_parts[2] + lift_self[..., None] * self_value.astype(jnp.float32)
    denominator = lift_prefix * prefix_parts[1] + lift_suffix * suffix_parts[1] + lift_self
    return numerator / denominator[..., None]

def reference(queries, new_kv, prefix_kv, suffix_kv, suffix_len, parents, out_weight, residual, steer_dict, steer_ids, steer_strength, norm_gain, norm_bias):
    score_scale = HEAD ** (-0.5)
    pre_keys = prefix_kv[:, 0].reshape(P_PRE, HEADS, HEAD)
    pre_values = prefix_kv[:, 1].reshape(P_PRE, HEADS, HEAD)
    block_rows = math.gcd(BEAMS, 64)

    def attend_block(row_start):
        query_rows = lax.dynamic_slice_in_dim(queries, row_start, block_rows, 0).reshape(block_rows, HEADS, HEAD)
        fresh_rows = lax.dynamic_slice_in_dim(new_kv, row_start, block_rows, 0)
        parent_ids = lax.dynamic_slice_in_dim(parents, row_start, block_rows, 0)
        parent_kv = jnp.take(suffix_kv, parent_ids, axis=0)
        live_len = jnp.take(suffix_len, parent_ids, axis=0)
        key_rows = parent_kv[:, :, 0].reshape(block_rows, S_SUF, HEADS, HEAD)
        value_rows = parent_kv[:, :, 1].reshape(block_rows, S_SUF, HEADS, HEAD)
        prefix_parts = prefix_part(query_rows, pre_keys, pre_values, score_scale)
        suffix_parts = suffix_part(query_rows, key_rows, value_rows, live_len, score_scale)
        new_keys = fresh_rows[:, 0].reshape(block_rows, HEADS, HEAD)
        new_values = fresh_rows[:, 1].reshape(block_rows, HEADS, HEAD)
        self_score = lax.optimization_barrier(jnp.sum(query_rows.astype(jnp.float32) * new_keys.astype(jnp.float32), axis=-1)) * score_scale
        merged = combine(prefix_parts, suffix_parts, self_score, new_values)
        return merged.reshape(block_rows, D).astype(jnp.bfloat16)
    starts = jnp.arange(0, BEAMS, block_rows, dtype=jnp.int32)
    attended = lax.map(attend_block, starts).reshape(BEAMS, D)
    projected = jnp.dot(attended, out_weight, preferred_element_type=jnp.float32)
    picked_rows = jnp.take(steer_dict, steer_ids, axis=0).astype(jnp.float32)
    steering = lax.optimization_barrier(jnp.sum(steer_strength[:, :, None] * picked_rows, axis=1))
    summed = residual.astype(jnp.float32) + projected + steering
    row_mean = lax.optimization_barrier(jnp.mean(summed, axis=1))
    centered = summed - row_mean[:, None]
    row_var = lax.optimization_barrier(jnp.mean(centered * centered, axis=1))
    normed = centered * lax.rsqrt(row_var + 1e-05)[:, None]
    return (normed * norm_gain[None, :] + norm_bias[None, :]).astype(jnp.bfloat16)
```

```python
import functools

import jax
import jax.numpy as jnp
from jax import lax
from jax.experimental import pallas as pl
from jax.experimental.pallas import tpu as pltpu
from jax.sharding import PartitionSpec as P

MESH = pl.DeviceIdType.MESH
F32, BF16, I32 = jnp.float32, jnp.bfloat16, jnp.int32
D = 10240
HEAD = 128
CAP = 2
X, Z, C = 4, 8, 2

NEG = -1e30
NT = (((1,), (1,)), ((), ()))
TN = (((0,), (0,)), ((), ()))


def iota(shape, dim):
    return lax.broadcasted_iota(I32, shape, dim)


def log2(n):
    return n.bit_length() - 1


def dot(a, b, dims=(((1,), (0,)), ((), ()))):
    return lax.dot_general(a, b, dims, preferred_element_type=F32)


def rows(start, size):
    return pl.ds(pl.multiple_of(start, size & -size), size)


class Exchange:
    def __init__(self, src, dst, n, me, peer_id, send, recv, chunk):
        self.src, self.dst, self.n, self.me = src, dst, n, me
        self.peer_id, self.send, self.recv, self.chunk = peer_id, send, recv, chunk

    def copy(self, k, to, out_at, in_at):
        return pltpu.make_async_remote_copy(
            src_ref=self.src.at[rows(out_at * self.chunk, self.chunk)],
            dst_ref=self.dst.at[rows(in_at * self.chunk, self.chunk)],
            send_sem=self.send.at[k],
            recv_sem=self.recv.at[k],
            device_id=self.peer_id(to),
            device_id_type=MESH,
        )

    def start(self):
        n, me = self.n, self.me

        def step(k, _):
            to = lax.rem(me + k, n)
            self.copy(k, to, to, me).start()
            return 0

        lax.fori_loop(1, n, step, 0)
        mine = rows(me * self.chunk, self.chunk)
        self.dst[mine] = self.src[mine]

    def wait(self):
        n, me = self.n, self.me

        def step(k, _):
            frm = lax.rem(me + n - k, n)
            self.copy(k, frm, frm, frm).wait_recv()
            return 0

        lax.fori_loop(1, n, step, 0)

    def drain(self):
        n, me = self.n, self.me

        def step(k, _):
            to = lax.rem(me + k, n)
            self.copy(k, to, to, me).wait_send()
            return 0

        lax.fori_loop(1, n, step, 0)


class Share(Exchange):
    def copy(self, k, to, out_at, in_at):
        return pltpu.make_async_remote_copy(
            src_ref=self.src,
            dst_ref=self.dst.at[in_at],
            send_sem=self.send.at[k],
            recv_sem=self.recv.at[k],
            device_id=self.peer_id(to),
            device_id_type=MESH,
        )

    def start(self):
        n, me = self.n, self.me

        def step(k, _):
            to = lax.rem(me + k, n)
            self.copy(k, to, to, me).start()
            return 0

        lax.fori_loop(1, n, step, 0)
        self.dst[me] = self.src[...]


class Ring:
    def __init__(self, view, n, me, peer_id, send, recv, split):
        self.view, self.n, self.me, self.peer_id = view, n, me, peer_id
        self.send, self.recv, self.split = send, recv, split
        self.steps = n // 2

    def moves(self, s):
        far = 2 * s == self.n
        if not far:
            return [(0, None), (1, None)]
        return [(0, 0), (1, 1)] if self.split else [(0, None)]

    def copy(self, s, way, part, index, to):
        ref = self.view(index, part)
        return pltpu.make_async_remote_copy(
            src_ref=ref,
            dst_ref=ref,
            send_sem=self.send.at[way, s - 1],
            recv_sem=self.recv.at[way, s - 1],
            device_id=self.peer_id(to),
            device_id_type=MESH,
        )

    def outgoing(self, s):
        n, me = self.n, self.me
        for way, part in self.moves(s):
            if way == 0:
                yield self.copy(s, way, part, lax.rem(me + n - s + 1, n), lax.rem(me + 1, n))
            else:
                yield self.copy(s, way, part, lax.rem(me + s - 1, n), lax.rem(me + n - 1, n))

    def start(self, s):
        for c in self.outgoing(s):
            c.start()

    def wait(self, s):
        n, me = self.n, self.me
        for way, part in self.moves(s):
            if way == 0:
                self.copy(s, way, part, lax.rem(me + n - s, n), lax.rem(me + 1, n)).wait_recv()
            else:
                self.copy(s, way, part, lax.rem(me + s, n), lax.rem(me + n - 1, n)).wait_recv()

    def drain(self):
        for s in range(1, self.steps + 1):
            for c in self.outgoing(s):
                c.wait_send()


def three_terms(value):
    top = value.astype(BF16).astype(F32)
    rest = value - top
    middle = rest.astype(BF16).astype(F32)
    return top, middle, rest - middle


def kernel(
    Y,
    q_ref, kn_ref, vn_ref, pk_ref, pv_ref, sk_ref, sv_ref, len_ref, par_ref,
    w_ref, res_ref, dict_ref, ids_ref, str_ref, gain_ref, bias_ref,
    out_ref,
    qs_a, q1_a, q2_a, q3_a, qs_b, q1_b, q2_b, q3_b,
    rs_a, r1_a, r2_a, r3_a, rs_b, r1_b, r2_b, r3_b,
    num, top1, den1, att_a, att_b, ag_a, ag_b, wbuf, base, acc, sib, st1, st2, g1, g2,
    ex_send, ex_recv, sh_send, sh_recv, y_send, y_recv, ws_send, ws_recv,
    az_send, az_recv, ax_send, ax_recv, bx_send, bx_recv, bz_send, bz_recv,
    pm_send, pm_recv, own_sem, sb_send, sb_recv,
):
    NX = X * C
    G = NX * Z
    S = G * CAP
    B, width = q_ref.shape
    half = width // 2
    heads = half // HEAD
    n_a = X * Z // Y
    W = w_ref.shape[0]
    R = res_ref.shape[1]
    RC = R // C
    scale = HEAD ** (-0.5)

    d = lax.axis_index("dp")
    y = lax.axis_index("tensor")
    c = lax.rem(d, C)
    p = lax.div(d, C)
    z = lax.rem(p, Z)
    x = lax.div(p, Z)
    xc = x * C + c

    def xc_id(i):
        return ((lax.div(i, C) * Z + z) * C + lax.rem(i, C), y)

    def z_id(i):
        return ((x * Z + i) * C + c, y)

    def x_id(i):
        return ((i * Z + z) * C + c, y)

    def y_id(i):
        return (d, i)

    sibling = (p * C + (1 - c), y)
    f_out = lax.rem(lax.div(p, n_a) + y, Y)
    p_out = f_out * n_a + lax.rem(p, n_a)
    to_block = (p_out * C + c, lax.div(p, n_a))
    from_y = lax.rem(lax.div(p, n_a) + Y - y, Y)
    p_in = y * n_a + lax.rem(p, n_a)
    from_block = (p_in * C + c, from_y)
    stays = jnp.logical_and(p_out == p, lax.div(p, n_a) == y)

    barrier = pltpu.get_barrier_semaphore()

    def hello(dev):
        pl.semaphore_signal(barrier, inc=1, device_id=dev, device_id_type=MESH)

    def greet(peer_id, n, me):
        def step(k, _):
            hello(peer_id(lax.rem(me + k, n)))
            return 0

        lax.fori_loop(1, n, step, 0)

    greet(xc_id, NX, xc)
    greet(z_id, Z, z)
    hello(y_id(lax.rem(y + 1, Y)))
    hello(y_id(lax.rem(y + Y - 1, Y)))

    @pl.when(jnp.logical_not(stays))
    def _():
        hello(from_block)

    r_bits = log2(CAP)
    slot = iota((S, 1), 0)
    rank_of = (slot & (CAP - 1)).astype(F32)
    group = slot >> r_bits
    xc_a, z_a = group >> log2(Z), group & (Z - 1)
    z_b, xc_b = group >> log2(NX), group & (NX - 1)

    def d_of(xc_, z_):
        return (((xc_ >> log2(C)) * Z + z_) * C + (xc_ & (C - 1))).astype(F32)

    d_a, d_b = d_of(xc_a, z_a), d_of(xc_b, z_b)
    before = (iota((B, B), 0) < iota((B, B), 1)).astype(BF16)

    def split_parents(par):
        par = par.astype(F32)
        src = jnp.floor((par + 0.5) * (1.0 / B))
        return src, par - src * B

    my_src, _ = split_parents(par_ref[pl.ds(d, 1), :])

    def slots_of(dest):
        hit = my_src == dest
        rank = dot(hit.astype(BF16), before)
        return (hit & (rank == rank_of)).astype(BF16)

    e_a, e_b = slots_of(d_a), slots_of(d_b)
    qs_a[...] = dot(e_a, q_ref[:, :half]).astype(BF16)
    qs_b[...] = dot(e_b, q_ref[:, half:]).astype(BF16)

    own_w = pltpu.make_async_copy(w_ref, wbuf.at[y, c], own_sem)
    own_w.start()

    pl.semaphore_wait(barrier, jnp.where(stays, 0, 1) + (NX - 1 + Z - 1 + 2))

    exchanges = []

    def exchange(src, dst, over_z, index, chunk):
        n, me, peer = (Z, z, z_id) if over_z else (NX, xc, xc_id)
        e = Exchange(src, dst, n, me, peer, ex_send.at[index], ex_recv.at[index], chunk)
        exchanges.append(e)
        return e

    ca, cb = Z * CAP, NX * CAP
    e1a = exchange(qs_a, q1_a, False, 0, ca)
    e1b = exchange(qs_b, q1_b, True, 1, cb)
    e2a = exchange(q2_a, q3_a, True, 2, cb)
    e2b = exchange(q2_b, q3_b, False, 3, ca)
    e3a = exchange(rs_a, r1_a, True, 4, cb)
    e3b = exchange(rs_b, r1_b, False, 5, ca)
    e4a = exchange(r2_a, r3_a, False, 6, ca)
    e4b = exchange(r2_b, r3_b, True, 7, cb)

    e1a.start()
    e1b.start()

    own_w.wait()
    wring = Ring(lambda i, part: wbuf.at[i, c], Y, y, y_id, y_send, y_recv, False)

    def to_sibling(index, at, core):
        ref = wbuf.at[index, core]
        return pltpu.make_async_remote_copy(
            src_ref=ref, dst_ref=ref, send_sem=ws_send.at[at], recv_sem=ws_recv.at[at],
            device_id=sibling, device_id_type=MESH,
        )

    handed = []

    def hand(offset):
        index = lax.rem(y + offset + Y, Y)
        at = len(handed)
        to_sibling(index, at, c).start()
        handed.append(index)

    wring.start(1)
    hand(0)

    def w_step(s):
        wring.wait(s)
        if s < wring.steps:
            wring.start(s + 1)
        for way, _ in wring.moves(s):
            hand(-s if way == 0 else s)

    for h in range(2 * heads):
        cols = slice(h * HEAD, (h + 1) * HEAD)
        qh = q_ref[:, cols]
        s_pre = dot(qh, pk_ref[:, cols], NT) * scale
        m_pre = jnp.max(s_pre, axis=1, keepdims=True)
        e_pre = jnp.exp(s_pre - m_pre)
        l_pre = jnp.sum(e_pre, axis=1, keepdims=True)
        o_pre = dot(e_pre.astype(BF16), pv_ref[:, cols])
        s_self = scale * jnp.sum(
            qh.astype(F32) * kn_ref[:, cols].astype(F32), axis=1, keepdims=True
        )
        m1 = jnp.maximum(m_pre, s_self)
        up, us = jnp.exp(m_pre - m1), jnp.exp(s_self - m1)
        num[:, cols] = up * o_pre + us * vn_ref[:, cols].astype(F32)
        top1[h] = jnp.broadcast_to(m1, (B, HEAD))
        den1[h] = jnp.broadcast_to(up * l_pre + us, (B, HEAD))

    out_i, in_j = iota((S, S), 0), iota((S, S), 1)

    def swap(n_out, n_in):
        g = out_i >> r_bits
        u, v = g >> log2(n_in), g & (n_in - 1)
        return (in_j == ((v * n_out + u) * CAP + (out_i & (CAP - 1)))).astype(BF16)

    to_b, to_a = swap(Z, NX), swap(NX, Z)

    e1a.wait()
    q2_a[...] = dot(to_b, q1_a[...]).astype(BF16)
    e2a.start()
    e1b.wait()
    q2_b[...] = dot(to_a, q1_b[...]).astype(BF16)
    e2b.start()
    w_step(1)

    src, off = split_parents(par_ref[...])
    group_of = iota((S, G), 1).astype(F32)
    keys = sk_ref.shape[0]
    T = keys // B
    beam_of = iota((B, keys), 1) >> log2(T)
    spread = (beam_of == iota((B, keys), 0)).astype(BF16)
    live = dot(len_ref[pl.ds(d, 1), :].astype(F32).astype(BF16), spread)
    live_cols = (iota((1, keys), 1) & (T - 1)).astype(F32) < live
    col_beam = (iota((1, keys), 1) >> log2(T)).astype(F32)
    here = d.astype(F32)

    def mask_of(dest):
        pick = (group_of == dest).astype(BF16)
        hit = dot(pick, src.astype(BF16)) == here
        rank = dot(hit.astype(BF16), before)
        chosen = (hit & (rank == rank_of)).astype(F32)
        offset = jnp.sum(chosen * dot(pick, off.astype(BF16)), axis=1, keepdims=True)
        there = jnp.sum(chosen, axis=1, keepdims=True) > 0.0
        offset = jnp.where(there, offset, -1.0)
        return (offset == col_beam) & live_cols

    feats = dict_ref.shape[1]
    step_f = min(feats, 128)
    base[...] = res_ref[...].astype(F32)

    def steer(i, _):
        at = i * step_f
        feature = iota((step_f, R), 0) + at
        s = jnp.zeros((step_f, R), F32)
        for k in range(ids_ref.shape[0]):
            s = s + jnp.where(feature == ids_ref[k : k + 1, :], str_ref[k : k + 1, :], 0.0)
        top, middle, _ = three_terms(s)
        part = dict_ref[:, rows(at, step_f)]
        base[...] += dot(part, top.astype(BF16)) + dot(part, middle.astype(BF16))
        return 0

    lax.fori_loop(0, feats // step_f, steer, 0)

    def attend(q3, mask, rs, first):
        lane = iota((S, HEAD), 1)
        extra = jnp.zeros((S, HEAD), F32)
        for i in range(heads):
            cols = slice((first + i) * HEAD, (first + i + 1) * HEAD)
            mine = slice(i * HEAD, (i + 1) * HEAD)
            s = dot(q3[:, mine], sk_ref[:, cols], NT) * scale
            s = jnp.where(mask, s, NEG)
            m = jnp.max(s, axis=1, keepdims=True)
            e = jnp.where(mask, jnp.exp(s - m), 0.0)
            l = jnp.maximum(jnp.sum(e, axis=1, keepdims=True), 1e-30)
            o = dot(e.astype(BF16), sv_ref[:, cols]) / l
            rs[:, mine] = o.astype(BF16)
            for k, term in enumerate(three_terms(m + jnp.log(l))):
                extra = jnp.where(lane == k * heads + i, term, extra)
        rs[:, half:] = extra.astype(BF16)

    mask_b = mask_of(d_b)
    e2a.wait()
    attend(q3_a, mask_b, rs_a, 0)
    e3a.start()
    mask_a = mask_of(d_a)
    e2b.wait()
    attend(q3_b, mask_a, rs_b, heads)
    e3b.start()
    if wring.steps > 1:
        w_step(2)

    e3a.wait()
    r2_a[...] = dot(to_a, r1_a[...]).astype(BF16)
    e4a.start()
    e3b.wait()
    r2_b[...] = dot(to_b, r1_b[...]).astype(BF16)
    e4b.start()
    if wring.steps > 2:
        w_step(3)

    def merge(e, r3, att, first):
        got = dot(e, r3[...], TN)
        for i in range(heads):
            h = first + i
            mine = slice(i * HEAD, (i + 1) * HEAD)
            lse = sum(
                got[:, half + k * heads + i : half + k * heads + i + 1] for k in range(3)
            )
            m1 = top1[h]
            m = jnp.maximum(m1, lse)
            a, b = jnp.exp(m1 - m), jnp.exp(lse - m)
            total = a * num[:, h * HEAD : (h + 1) * HEAD] + b * got[:, mine]
            att[:, mine] = (total / (a * den1[h] + b)).astype(BF16)

    def block_a(xi, zi):
        return ag_a.at[rows((xi * Z + zi) * B, B)]

    def block_b(xi, zi):
        return ag_b.at[zi, xi]

    def place(att, block, at, outward):
        dst = block(lax.div(p_out, Z), lax.rem(p_out, Z)) if outward else block(x, z)
        return pltpu.make_async_remote_copy(
            src_ref=att, dst_ref=dst, send_sem=pm_send.at[at], recv_sem=pm_recv.at[at],
            device_id=to_block, device_id_type=MESH,
        )

    def send_block(att, block, at):
        out = place(att, block, at, True)

        @pl.when(stays)
        def _():
            block(x, z)[...] = att[...]

        @pl.when(jnp.logical_not(stays))
        def _():
            out.start()

    def take_block(att, block, at):
        out, into = place(att, block, at, True), place(att, block, at, False)

        @pl.when(jnp.logical_not(stays))
        def _():
            into.wait_recv()
            out.wait_send()

    e4a.wait()
    merge(e_a, r3_a, att_a, 0)
    send_block(att_a, block_a, 0)
    e4b.wait()
    merge(e_b, r3_b, att_b, heads)
    send_block(att_b, block_b, 1)

    hz, hx = Z * B // 2, X // 2
    az = Ring(lambda i, part: block_a(x, i), Z, z, z_id, az_send, az_recv, False)

    def set_a(i, part):
        if part is None:
            return ag_a.at[rows(i * Z * B, Z * B)]
        return ag_a.at[rows(i * Z * B + part * hz, hz)]

    ax = Ring(set_a, X, x, x_id, ax_send, ax_recv, True)
    bx = Ring(lambda i, part: block_b(i, z), X, x, x_id, bx_send, bx_recv, False)

    def set_b(i, part):
        if part is None:
            return ag_b.at[i]
        return ag_b.at[i, pl.ds(part * hx, hx)]

    bz = Ring(set_b, Z, z, z_id, bz_send, bz_recv, True)

    take_block(att_a, block_a, 0)
    az.start(1)
    take_block(att_b, block_b, 1)
    bx.start(1)
    acc[...] = jnp.zeros_like(acc)
    if wring.steps > 3:
        w_step(4)
    for s in range(1, bx.steps + 1):
        bx.wait(s)
        if s < bx.steps:
            bx.start(s + 1)
        if s < az.steps:
            az.wait(s)
            az.start(s + 1)
    bz.start(1)
    for s in range(bx.steps + 1, az.steps):
        az.wait(s)
        az.start(s + 1)
    az.wait(az.steps)
    ax.start(1)

    for at, index in enumerate(handed):
        to_sibling(index, at, 1 - c).wait_recv()

    n_f = Z // n_a

    def slice_a(f):
        return ag_a[rows(f * n_a * B, n_a * B), :]

    def slice_b(f):
        zi = lax.rem(f, n_f) * n_a
        got = ag_b[pl.ds(zi, n_a), lax.div(f, n_f)]
        return got.reshape(n_a * B, half)

    def multiply(f, part, at):
        ys = lax.rem(f - y + Y, Y)
        weights = wbuf[ys, :, :, at : at + half].reshape(C * W, half)
        acc[...] += dot(weights, part, NT)

    def multiply_a(xi):
        for k in range(n_f):
            f = xi * n_f + k
            multiply(f, slice_a(f), 0)

    multiply_a(x)
    bz.wait(1)
    bz.start(2) if bz.steps > 1 else None
    ax.wait(1)
    ax.start(2) if ax.steps > 1 else None
    if X > 2:
        multiply_a(lax.rem(x + 1, X))
        multiply_a(lax.rem(x + X - 1, X))
    for s in range(2, bz.steps + 1):
        bz.wait(s)
        if s < bz.steps:
            bz.start(s + 1)
    for s in range(2, ax.steps + 1):
        ax.wait(s)
    multiply_a(lax.rem(x + X // 2, X))

    def multiply_b(f, _):
        multiply(f, slice_b(f), half)
        return 0

    lax.fori_loop(0, Y, multiply_b, 0)

    swap_out = pltpu.make_async_remote_copy(
        src_ref=acc.at[rows((1 - c) * W, W)], dst_ref=sib,
        send_sem=sb_send, recv_sem=sb_recv, device_id=sibling, device_id_type=MESH,
    )
    swap_out.start()
    ri, ci = iota((RC, R), 0), iota((RC, R), 1)
    block_no = sum((ri >= B * k).astype(I32) for k in range(1, n_a))
    inner = ri - block_no * B

    def spot(cls):
        return (ci == (block_no * C + cls) * B + inner).astype(F32)

    def put(value, cls):
        return lax.dot_general(
            value, spot(cls), (((1,), (0,)), ((), ())),
            preferred_element_type=F32, precision=lax.Precision.HIGHEST,
        )

    summed = base[...] + put(acc[rows(c * W, W), :], c)
    swap_out.wait_recv()
    summed = summed + put(sib[...], 1 - c)

    def join(got, n_each):
        n = got.shape[0]
        means, squares = got[:, 0:1, :], got[:, 1:2, :]
        mean = jnp.sum(means, axis=0) * (1.0 / n)
        away = means - mean[None]
        square = jnp.sum(squares, axis=0) + n_each * jnp.sum(away * away, axis=0)
        return mean, square

    row_no = iota((8, R), 0)

    def pack(mean, square):
        return jnp.where(row_no == 0, mean, jnp.where(row_no == 1, square, 0.0))

    mean = jnp.sum(summed, axis=0, keepdims=True) * (1.0 / W)
    away = summed - mean
    st1[...] = pack(mean, jnp.sum(away * away, axis=0, keepdims=True))
    s1 = Share(st1, g1, NX, xc, xc_id, sh_send.at[0], sh_recv.at[0], 1)
    s1.start()
    eye = iota((W, W), 0) == iota((W, W), 1)
    gain = jnp.sum(jnp.where(eye, gain_ref[...], 0.0), axis=1, keepdims=True)
    bias = jnp.sum(jnp.where(eye, bias_ref[...], 0.0), axis=1, keepdims=True)
    s1.wait()
    st2[...] = pack(*join(g1[...], float(W)))
    s2 = Share(st2, g2, Z, z, z_id, sh_send.at[1], sh_recv.at[1], 1)
    s2.start()
    s2.wait()
    mean, square = join(g2[...], float(W * NX))
    var = square * (1.0 / (W * NX * Z))
    normed = (summed - mean) * lax.rsqrt(var + 1e-5)
    out_ref[...] = (normed * gain + bias).astype(BF16)

    for e in exchanges:
        e.drain()
    s1.drain()
    s2.drain()
    for ring in (wring, az, ax, bx, bz):
        ring.drain()
    for at, index in enumerate(handed):
        to_sibling(index, at, c).wait_send()
    swap_out.wait_send()


def on_device(
    queries, new_kv, prefix_kv, suffix_kv, suffix_len, parents, out_weight, residual,
    steer_dict, steer_ids, steer_strength, norm_gain, norm_bias,
):
    G = lax.axis_size("dp")
    Y = lax.axis_size("tensor")
    NX = X * C
    S = G * CAP
    B, width = queries.shape
    half = width // 2
    heads2 = width // HEAD
    T = suffix_kv.shape[1]
    W = out_weight.shape[1]
    R = residual.shape[0]
    RC = R // C
    VM = pltpu.VMEM
    DMA = pltpu.SemaphoreType.DMA
    sent = half + HEAD
    args = (
        queries,
        new_kv[:, 0], new_kv[:, 1],
        prefix_kv[:, 0], prefix_kv[:, 1],
        suffix_kv[:, :, 0].reshape(B * T, width), suffix_kv[:, :, 1].reshape(B * T, width),
        suffix_len.reshape(G, B), parents.reshape(G, B),
        out_weight.T, residual.T, steer_dict.T, steer_ids.T, steer_strength.T,
        norm_gain[None], norm_bias[None],
    )
    big = max(NX, Z)
    scratch = (
        [VM((S, half), BF16)] * 8
        + [VM((S, sent), BF16)] * 8
        + [
            VM((B, width), F32), VM((heads2, B, HEAD), F32), VM((heads2, B, HEAD), F32),
            VM((B, half), BF16), VM((B, half), BF16),
            VM((X * Z * B, half), BF16), VM((Z, X, B, half), BF16),
            VM((Y, C, W, width), BF16),
            VM((W, R), F32), VM((C * W, RC), F32), VM((W, RC), F32),
            VM((8, R), F32), VM((8, R), F32), VM((NX, 8, R), F32), VM((Z, 8, R), F32),
        ]
        + [DMA((8, big))] * 2
        + [DMA((2, big))] * 2
        + [DMA((2, Y // 2))] * 2
        + [DMA((Y,))] * 2
        + [DMA((2, Z // 2))] * 2
        + [DMA((2, X // 2))] * 2
        + [DMA((2, X // 2))] * 2
        + [DMA((2, Z // 2))] * 2
        + [DMA((2,))] * 2
        + [DMA] * 3
    )
    out = pl.pallas_call(
        functools.partial(kernel, Y),
        out_shape=jax.ShapeDtypeStruct((W, R), BF16),
        in_specs=[pl.BlockSpec(memory_space=VM)] * len(args),
        out_specs=pl.BlockSpec(memory_space=VM),
        scratch_shapes=scratch,
        compiler_params=pltpu.CompilerParams(
            collective_id=0, has_side_effects=True, vmem_limit_bytes=56 * 1024 * 1024
        ),
        name="beam_step",
    )(*args)
    return out.T


def solution(mesh):
    placed = (
        P("dp", "tensor"),
        P("dp", None, "tensor"),
        P(None, None, "tensor"),
        P("dp", None, None, "tensor"),
        P(),
        P(),
        P("tensor", "dp"),
        P("tensor", "dp"),
        P(None, "dp"),
        P("tensor", None),
        P("tensor", None),
        P("dp"),
        P("dp"),
    )
    return jax.shard_map(
        on_device, mesh=mesh, in_specs=placed, out_specs=P("tensor", "dp"), check_vma=False
    )
```

```python
import functools

import jax
import jax.numpy as jnp
from jax import lax
from jax.experimental import pallas as pl
from jax.experimental.pallas import tpu as pltpu
from jax.sharding import PartitionSpec as P

MESH = pl.DeviceIdType.MESH
F32, BF16, I32 = jnp.float32, jnp.bfloat16, jnp.int32
D = 10240
HEAD = 128
CAP = 2
PACK = 16
X, Z, C = 4, 8, 2

NEG = -1e30
NT = (((1,), (1,)), ((), ()))
TN = (((0,), (0,)), ((), ()))


def iota(shape, dim):
    return lax.broadcasted_iota(I32, shape, dim)


def log2(n):
    return n.bit_length() - 1


def dot(a, b, dims=(((1,), (0,)), ((), ()))):
    return lax.dot_general(a, b, dims, preferred_element_type=F32)


def rows(start, size):
    return pl.ds(pl.multiple_of(start, size & -size), size)


def heads_of(width):
    heads = width // HEAD
    first = max(1, heads * 3 // 5)
    return first * HEAD, first, heads - first


class Exchange:
    def __init__(self, src, dst, n, me, peer_id, send, recv, chunk):
        self.src, self.dst, self.n, self.me = src, dst, n, me
        self.peer_id, self.send, self.recv, self.chunk = peer_id, send, recv, chunk

    def copy(self, k, to, out_at, in_at):
        return pltpu.make_async_remote_copy(
            src_ref=self.src.at[rows(out_at * self.chunk, self.chunk)],
            dst_ref=self.dst.at[rows(in_at * self.chunk, self.chunk)],
            send_sem=self.send.at[k],
            recv_sem=self.recv.at[k],
            device_id=self.peer_id(to),
            device_id_type=MESH,
        )

    def start(self):
        n, me = self.n, self.me

        def step(k, _):
            to = lax.rem(me + k, n)
            self.copy(k, to, to, me).start()
            return 0

        lax.fori_loop(1, n, step, 0)
        mine = rows(me * self.chunk, self.chunk)
        self.dst[mine] = self.src[mine]

    def wait(self):
        n, me = self.n, self.me

        def step(k, _):
            frm = lax.rem(me + n - k, n)
            self.copy(k, frm, frm, frm).wait_recv()
            return 0

        lax.fori_loop(1, n, step, 0)

    def drain(self):
        n, me = self.n, self.me

        def step(k, _):
            to = lax.rem(me + k, n)
            self.copy(k, to, to, me).wait_send()
            return 0

        lax.fori_loop(1, n, step, 0)


class Share(Exchange):
    def copy(self, k, to, out_at, in_at):
        return pltpu.make_async_remote_copy(
            src_ref=self.src,
            dst_ref=self.dst.at[in_at],
            send_sem=self.send.at[k],
            recv_sem=self.recv.at[k],
            device_id=self.peer_id(to),
            device_id_type=MESH,
        )

    def start(self):
        n, me = self.n, self.me

        def step(k, _):
            to = lax.rem(me + k, n)
            self.copy(k, to, to, me).start()
            return 0

        lax.fori_loop(1, n, step, 0)
        self.dst[me] = self.src[...]


class Ring:
    def __init__(self, view, n, me, peer_id, send, recv, split=False, last_way=0):
        self.view, self.n, self.me, self.peer_id = view, n, me, peer_id
        self.send, self.recv, self.split, self.last_way = send, recv, split, last_way
        self.steps = n // 2

    def moves(self, s):
        if s < 1 or s > self.steps:
            return []
        if 2 * s < self.n:
            return [(0, None), (1, None)]
        return [(0, 0), (1, 1)] if self.split else [(self.last_way, None)]

    def copy(self, s, way, part, index):
        ref = self.view(index, part)
        to = lax.rem(self.me + 1, self.n) if way == 0 else lax.rem(self.me + self.n - 1, self.n)
        return pltpu.make_async_remote_copy(
            src_ref=ref,
            dst_ref=ref,
            send_sem=self.send.at[way, s - 1],
            recv_sem=self.recv.at[way, s - 1],
            device_id=self.peer_id(to),
            device_id_type=MESH,
        )

    def at(self, offset):
        return lax.rem(self.me + offset + self.n, self.n)

    def outgoing(self, s):
        for way, part in self.moves(s):
            yield self.copy(s, way, part, self.at(1 - s if way == 0 else s - 1))

    def start(self, s):
        for c in self.outgoing(s):
            c.start()

    def wait(self, s):
        for way, part in self.moves(s):
            self.copy(s, way, part, self.at(-s if way == 0 else s)).wait_recv()

    def drain(self):
        for s in range(1, self.steps + 1):
            for c in self.outgoing(s):
                c.wait_send()


def three_terms(value):
    top = value.astype(BF16).astype(F32)
    rest = value - top
    middle = rest.astype(BF16).astype(F32)
    return top, middle, rest - middle


def kernel(
    Y,
    q_ref, new_hbm, pre_hbm, suf_hbm, par_ref,
    w_hbm, res_ref, dict_hbm, ids_ref, str_ref, gain_ref, bias_ref,
    out_ref,
    qs_a, q1_a, q2_a, q3_a, qs_b, q1_b, q2_b, q3_b,
    rs_a, r1_a, r2_a, r3_a, rs_b, r1_b, r2_b, r3_b,
    new_raw, pre_raw, suf_raw, sk_ref, sv_ref, dict_ref,
    num, top1, den1, att_a, att_b, ag_a, ag_b, wbuf, base, acc, sib, st1, st2, g1, g2,
    ex_send, ex_recv, sh_send, sh_recv, y_send, y_recv, ws_send, ws_recv,
    az_send, az_recv, ax_send, ax_recv, bx_send, bx_recv, bz_send, bz_recv,
    pm_send, pm_recv, in_sem, sb_send, sb_recv,
):
    NX = X * C
    G = NX * Z
    S = G * CAP
    B, width = q_ref.shape
    split, heads_a, heads_b = heads_of(width)
    wide = width - split
    n_a = X * Z // Y
    n_f = Z // n_a
    W = w_hbm.shape[0]
    R = res_ref.shape[1]
    RC = R // C
    scale = HEAD ** (-0.5)

    d = lax.axis_index("dp")
    y = lax.axis_index("tensor")
    c = lax.rem(d, C)
    p = lax.div(d, C)
    z = lax.rem(p, Z)
    x = lax.div(p, Z)
    xc = x * C + c

    def xc_id(i):
        return ((lax.div(i, C) * Z + z) * C + lax.rem(i, C), y)

    def z_id(i):
        return ((x * Z + i) * C + c, y)

    def x_id(i):
        return ((i * Z + z) * C + c, y)

    def y_id(i):
        return (d, i)

    sibling = (p * C + (1 - c), y)
    shift = (Z - n_a) // 2 // n_f * n_f
    t_out = lax.div(p, n_a)
    delta = lax.rem(y - t_out + Y, Y)
    x_out = lax.rem(x + lax.div(delta, n_f) + X // 2, X)
    z_first = lax.rem(t_out, n_f) * n_a
    z_out = lax.rem(z_first + n_f * lax.rem(z, n_a) - shift + lax.rem(delta, n_f) + Z, Z)
    to_block = ((x_out * Z + z_out) * C + c, t_out)

    def y_of(xi, bit):
        jump = lax.rem(xi - lax.div(y, n_f) + X + X // 2, X)
        return lax.rem(y + n_f * jump + bit, Y)

    z_low = lax.rem(y, n_f) * n_a
    bit_in = lax.rem(z, n_f)
    a_in = lax.div(lax.rem(z - bit_in - z_low + shift + Z, Z), n_f)
    from_block = ((lax.div(y, n_f) * Z + z_low + a_in) * C + c, y_of(x, bit_in))

    barrier = pltpu.get_barrier_semaphore()

    def hello(dev):
        pl.semaphore_signal(barrier, inc=1, device_id=dev, device_id_type=MESH)

    def greet(peer_id, n, me):
        def step(k, _):
            hello(peer_id(lax.rem(me + k, n)))
            return 0

        lax.fori_loop(1, n, step, 0)

    greet(xc_id, NX, xc)
    greet(z_id, Z, z)
    hello(y_id(lax.rem(y + 1, Y)))
    hello(y_id(lax.rem(y + Y - 1, Y)))

    hello(from_block)

    loads = [
        pltpu.make_async_copy(a, b, in_sem.at[i])
        for i, (a, b) in enumerate((
            (w_hbm, wbuf.at[y, c]), (new_hbm, new_raw), (pre_hbm, pre_raw),
            (suf_hbm, suf_raw), (dict_hbm, dict_ref),
        ))
    ]
    for load in loads:
        load.start()

    r_bits = log2(CAP)
    slot = iota((S, 1), 0)
    rank_of = (slot & (CAP - 1)).astype(F32)
    group = slot >> r_bits
    xc_a, z_a = group >> log2(Z), group & (Z - 1)
    z_b, xc_b = group >> log2(NX), group & (NX - 1)

    def d_of(xc_, z_):
        return (((xc_ >> log2(C)) * Z + z_) * C + (xc_ & (C - 1))).astype(F32)

    d_a, d_b = d_of(xc_a, z_a), d_of(xc_b, z_b)
    before = (iota((B, B), 0) < iota((B, B), 1)).astype(BF16)

    def split_parents(par):
        par = par.astype(F32)
        both = jnp.floor(par * (1.0 / PACK))
        src = jnp.floor((both + 0.5) * (1.0 / B))
        return src, both - src * B, par - both * PACK

    my_src, _, my_len = split_parents(par_ref[pl.ds(d, 1), :])

    def slots_of(dest):
        hit = my_src == dest
        rank = dot(hit.astype(BF16), before)
        return (hit & (rank == rank_of)).astype(BF16)

    e_a, e_b = slots_of(d_a), slots_of(d_b)
    qs_a[...] = dot(e_a, q_ref[:, :split]).astype(BF16)
    qs_b[...] = dot(e_b, q_ref[:, split:]).astype(BF16)

    pl.semaphore_wait(barrier, NX - 1 + Z - 1 + 3)

    exchanges = []

    def exchange(src, dst, over_z, index, chunk):
        n, me, peer = (Z, z, z_id) if over_z else (NX, xc, xc_id)
        e = Exchange(src, dst, n, me, peer, ex_send.at[index], ex_recv.at[index], chunk)
        exchanges.append(e)
        return e

    ca, cb = Z * CAP, NX * CAP
    e1a = exchange(qs_a, q1_a, False, 0, ca)
    e1b = exchange(qs_b, q1_b, True, 1, cb)
    e2a = exchange(q2_a, q3_a, True, 2, cb)
    e2b = exchange(q2_b, q3_b, False, 3, ca)
    e3a = exchange(rs_a, r1_a, True, 4, cb)
    e3b = exchange(rs_b, r1_b, False, 5, ca)
    e4a = exchange(r2_a, r3_a, False, 6, ca)
    e4b = exchange(r2_b, r3_b, True, 7, cb)

    e1a.start()
    e1b.start()

    def w_block(i, part):
        if part is None:
            return wbuf.at[i, c]
        return wbuf.at[i, c, pl.ds(part * (W // 2), W // 2)]

    loads[0].wait()
    wring = Ring(w_block, Y, y, y_id, y_send, y_recv, True)

    def to_sibling(index, at, core):
        ref = wbuf.at[index, core]
        return pltpu.make_async_remote_copy(
            src_ref=ref, dst_ref=ref, send_sem=ws_send.at[at], recv_sem=ws_recv.at[at],
            device_id=sibling, device_id_type=MESH,
        )

    handed = []

    def hand(offset):
        index = lax.rem(y + offset + Y, Y)
        at = len(handed)
        to_sibling(index, at, c).start()
        handed.append(index)

    wring.start(1)
    hand(0)

    def w_step(s):
        wring.wait(s)
        if s < wring.steps:
            wring.start(s + 1)
        hand(-s)
        if 2 * s < Y:
            hand(s)

    loads[1].wait()
    loads[2].wait()
    for h in range(heads_a + heads_b):
        cols = slice(h * HEAD, (h + 1) * HEAD)
        qh = q_ref[:, cols]
        pre = pre_raw[:, :, cols].astype(F32)
        new = new_raw[:, :, cols].astype(F32)
        s_pre = dot(qh, pre[:, 0].astype(BF16), NT) * scale
        m_pre = jnp.max(s_pre, axis=1, keepdims=True)
        e_pre = jnp.exp(s_pre - m_pre)
        l_pre = jnp.sum(e_pre, axis=1, keepdims=True)
        o_pre = dot(e_pre.astype(BF16), pre[:, 1].astype(BF16))
        s_self = scale * jnp.sum(qh.astype(F32) * new[:, 0], axis=1, keepdims=True)
        m1 = jnp.maximum(m_pre, s_self)
        up, us = jnp.exp(m_pre - m1), jnp.exp(s_self - m1)
        num[:, cols] = up * o_pre + us * new[:, 1]
        top1[h] = jnp.broadcast_to(m1, (B, HEAD))
        den1[h] = jnp.broadcast_to(up * l_pre + us, (B, HEAD))

    out_i, in_j = iota((S, S), 0), iota((S, S), 1)

    def swap(n_out, n_in):
        g = out_i >> r_bits
        u, v = g >> log2(n_in), g & (n_in - 1)
        return (in_j == ((v * n_out + u) * CAP + (out_i & (CAP - 1)))).astype(BF16)

    to_b, to_a = swap(Z, NX), swap(NX, Z)

    e1a.wait()
    q2_a[...] = dot(to_b, q1_a[...]).astype(BF16)
    e2a.start()
    e1b.wait()
    q2_b[...] = dot(to_a, q1_b[...]).astype(BF16)
    e2b.start()

    keys = sk_ref.shape[0]
    loads[3].wait()
    for h in range(heads_a + heads_b):
        cols = slice(h * HEAD, (h + 1) * HEAD)
        pair = suf_raw[:, :, :, cols].astype(F32)
        sk_ref[:, cols] = pair[:, :, 0].reshape(keys, HEAD).astype(BF16)
        sv_ref[:, cols] = pair[:, :, 1].reshape(keys, HEAD).astype(BF16)

    src, off, _ = split_parents(par_ref[...])
    group_of = iota((S, G), 1).astype(F32)
    T = keys // B
    beam_of = iota((B, keys), 1) >> log2(T)
    spread = (beam_of == iota((B, keys), 0)).astype(BF16)
    live = dot(my_len.astype(BF16), spread)
    live_cols = (iota((1, keys), 1) & (T - 1)).astype(F32) < live
    col_beam = (iota((1, keys), 1) >> log2(T)).astype(F32)
    here = d.astype(F32)

    def mask_of(dest):
        pick = (group_of == dest).astype(BF16)
        hit = dot(pick, src.astype(BF16)) == here
        rank = dot(hit.astype(BF16), before)
        chosen = (hit & (rank == rank_of)).astype(F32)
        offset = jnp.sum(chosen * dot(pick, off.astype(BF16)), axis=1, keepdims=True)
        there = jnp.sum(chosen, axis=1, keepdims=True) > 0.0
        offset = jnp.where(there, offset, -1.0)
        return (offset == col_beam) & live_cols

    feats = dict_ref.shape[1]
    step_f = min(feats, 128)
    base[...] = res_ref[...].astype(F32)
    loads[4].wait()

    def steer(i, _):
        at = i * step_f
        feature = iota((step_f, R), 0) + at
        s = jnp.zeros((step_f, R), F32)
        for k in range(ids_ref.shape[0]):
            s = s + jnp.where(feature == ids_ref[k : k + 1, :], str_ref[k : k + 1, :], 0.0)
        top, middle, _ = three_terms(s)
        part = dict_ref[:, rows(at, step_f)]
        base[...] += dot(part, top.astype(BF16)) + dot(part, middle.astype(BF16))
        return 0

    lax.fori_loop(0, feats // step_f, steer, 0)

    def attend(q3, mask, rs, first, heads):
        lane = iota((S, HEAD), 1)
        extra = jnp.zeros((S, HEAD), F32)
        for i in range(heads):
            cols = slice((first + i) * HEAD, (first + i + 1) * HEAD)
            mine = slice(i * HEAD, (i + 1) * HEAD)
            s = dot(q3[:, mine], sk_ref[:, cols], NT) * scale
            s = jnp.where(mask, s, NEG)
            m = jnp.max(s, axis=1, keepdims=True)
            e = jnp.where(mask, jnp.exp(s - m), 0.0)
            l = jnp.maximum(jnp.sum(e, axis=1, keepdims=True), 1e-30)
            o = dot(e.astype(BF16), sv_ref[:, cols]) / l
            rs[:, mine] = o.astype(BF16)
            for k, term in enumerate(three_terms(m + jnp.log(l))):
                extra = jnp.where(lane == k * heads + i, term, extra)
        rs[:, heads * HEAD :] = extra.astype(BF16)

    mask_b, mask_a = mask_of(d_b), mask_of(d_a)
    w_step(1)
    e2a.wait()
    attend(q3_a, mask_b, rs_a, 0, heads_a)
    e3a.start()
    e2b.wait()
    attend(q3_b, mask_a, rs_b, heads_a, heads_b)
    e3b.start()

    e3a.wait()
    r2_a[...] = dot(to_a, r1_a[...]).astype(BF16)
    e4a.start()
    e3b.wait()
    r2_b[...] = dot(to_b, r1_b[...]).astype(BF16)
    e4b.start()
    if wring.steps > 1:
        w_step(2)

    def merge(e, r3, att, first, heads):
        got = dot(e, r3[...], TN)
        for i in range(heads):
            h = first + i
            mine = slice(i * HEAD, (i + 1) * HEAD)
            extra = heads * HEAD + i
            lse = sum(got[:, extra + k * heads : extra + k * heads + 1] for k in range(3))
            m1 = top1[h]
            m = jnp.maximum(m1, lse)
            a, b = jnp.exp(m1 - m), jnp.exp(lse - m)
            total = a * num[:, h * HEAD : (h + 1) * HEAD] + b * got[:, mine]
            att[:, mine] = (total / (a * den1[h] + b)).astype(BF16)

    def block_a(xi, zi):
        return ag_a.at[xi, lax.div(zi, n_f), lax.rem(zi, n_f)]

    def block_b(xi, zi):
        return ag_b.at[xi, lax.div(zi, n_f), lax.rem(zi, n_f)]

    def place(att, block, at, outward):
        return pltpu.make_async_remote_copy(
            src_ref=att, dst_ref=block(x_out, z_out) if outward else block(x, z),
            send_sem=pm_send.at[at], recv_sem=pm_recv.at[at],
            device_id=to_block, device_id_type=MESH,
        )

    e4a.wait()
    merge(e_a, r3_a, att_a, 0, heads_a)
    place(att_a, block_a, 0, True).start()
    e4b.wait()
    merge(e_b, r3_b, att_b, heads_a, heads_b)
    place(att_b, block_b, 1, True).start()
    if wring.steps > 2:
        w_step(3)

    class Spread:
        def __init__(self, along, across):
            self.along, self.across = along, across

        def round(self, r):
            if r:
                self.along.wait(r)
            self.along.start(r + 1)
            fresh = [0] if r == 0 else [-r, r][: 1 if 2 * r == self.along.n else 2]
            if r <= self.along.steps:
                for o in fresh:
                    self.across[o].start(1)
            for o, ring in self.across.items():
                step = r - abs(o)
                if step > 0:
                    ring.wait(step)
                    ring.start(step + 1)

        def drain(self):
            self.along.drain()
            for ring in self.across.values():
                ring.drain()

    def offsets(n):
        return [0] + [o for k in range(1, n // 2 + 1) for o in ([-k, k] if 2 * k < n else [-k])]

    spread_a = Spread(
        Ring(lambda i, part: block_a(x, i), Z, z, z_id, az_send, az_recv),
        {
            o: Ring(
                lambda i, part, o=o: block_a(i, lax.rem(z + o + Z, Z)),
                X, x, x_id, ax_send.at[k], ax_recv.at[k], last_way=k % 2,
            )
            for k, o in enumerate(offsets(Z))
        },
    )
    spread_b = Spread(
        Ring(lambda i, part: block_b(i, z), X, x, x_id, bx_send, bx_recv),
        {
            o: Ring(
                lambda i, part, o=o: block_b(lax.rem(x + o + X, X), i),
                Z, z, z_id, bz_send.at[k], bz_recv.at[k], last_way=1 - k % 2,
            )
            for k, o in enumerate(offsets(X))
        },
    )
    rounds = (X + Z) // 2

    def multiply(xi, first):
        for bit in range(n_f):
            ys = y_of(xi, bit)
            for ag, at, size in ((ag_a, 0, split), (ag_b, split, wide)):
                weights = wbuf[ys, :, :, at : at + size].reshape(C * W, size)
                part = dot(weights, ag[xi, :, bit].reshape(n_a * B, size), NT)
                if first and bit == 0 and at == 0:
                    acc[...] = part
                else:
                    acc[...] += part

    def weights_here():
        for at, index in enumerate(handed):
            to_sibling(index, at, 1 - c).wait_recv()

    place(att_a, block_a, 0, False).wait_recv()
    place(att_b, block_b, 1, False).wait_recv()
    for r in range(rounds + 1):
        spread_a.round(r)
        spread_b.round(r)
        if r == 0 and wring.steps > 3:
            w_step(4)
        if r == Z // 2:
            weights_here()
        if r >= Z // 2:
            k = r - Z // 2
            multiply(lax.rem(x + k, X), k == 0)
            if 0 < 2 * k < X:
                multiply(lax.rem(x + X - k, X), False)

    swap_out = pltpu.make_async_remote_copy(
        src_ref=acc.at[rows((1 - c) * W, W)], dst_ref=sib,
        send_sem=sb_send, recv_sem=sb_recv, device_id=sibling, device_id_type=MESH,
    )
    swap_out.start()
    ri, ci = iota((RC, R), 0), iota((RC, R), 1)
    turn = n_a - lax.rem(y, n_f) * (n_a // n_f) + shift // n_f
    block_no = sum((ri >= B * k).astype(I32) for k in range(1, n_a))
    inner = ri - block_no * B
    place_no = (block_no + turn) & (n_a - 1)

    def spot(cls):
        return (ci == (place_no * C + cls) * B + inner).astype(F32)

    def put(value, cls):
        return lax.dot_general(
            value, spot(cls), (((1,), (0,)), ((), ())),
            preferred_element_type=F32, precision=lax.Precision.HIGHEST,
        )

    summed = base[...] + put(acc[rows(c * W, W), :], c)
    swap_out.wait_recv()
    summed = summed + put(sib[...], 1 - c)

    def join(got, n_each):
        n = got.shape[0]
        means, squares = got[:, 0:1, :], got[:, 1:2, :]
        mean = jnp.sum(means, axis=0) * (1.0 / n)
        away = means - mean[None]
        square = jnp.sum(squares, axis=0) + n_each * jnp.sum(away * away, axis=0)
        return mean, square

    row_no = iota((8, R), 0)

    def pack(mean, square):
        return jnp.where(row_no == 0, mean, jnp.where(row_no == 1, square, 0.0))

    mean = jnp.sum(summed, axis=0, keepdims=True) * (1.0 / W)
    away = summed - mean
    st1[...] = pack(mean, jnp.sum(away * away, axis=0, keepdims=True))
    s1 = Share(st1, g1, NX, xc, xc_id, sh_send.at[0], sh_recv.at[0], 1)
    s1.start()
    eye = iota((W, W), 0) == iota((W, W), 1)
    gain = jnp.sum(jnp.where(eye, gain_ref[...], 0.0), axis=1, keepdims=True)
    bias = jnp.sum(jnp.where(eye, bias_ref[...], 0.0), axis=1, keepdims=True)
    s1.wait()
    st2[...] = pack(*join(g1[...], float(W)))
    s2 = Share(st2, g2, Z, z, z_id, sh_send.at[1], sh_recv.at[1], 1)
    s2.start()
    s2.wait()
    mean, square = join(g2[...], float(W * NX))
    var = square * (1.0 / (W * NX * Z))
    normed = (summed - mean) * lax.rsqrt(var + 1e-5)
    out_ref[...] = (normed * gain + bias).astype(BF16)

    for e in exchanges:
        e.drain()
    s1.drain()
    s2.drain()
    for ring in (wring, spread_a, spread_b):
        ring.drain()
    place(att_a, block_a, 0, True).wait_send()
    place(att_b, block_b, 1, True).wait_send()
    for at, index in enumerate(handed):
        to_sibling(index, at, c).wait_send()
    swap_out.wait_send()


def on_device(
    queries, new_kv, prefix_kv, suffix_kv, suffix_len, parents, out_weight, residual,
    steer_dict, steer_ids, steer_strength, norm_gain, norm_bias,
):
    G = lax.axis_size("dp")
    Y = lax.axis_size("tensor")
    NX = X * C
    S = G * CAP
    B, width = queries.shape
    split, heads_a, heads_b = heads_of(width)
    wide = width - split
    heads2 = width // HEAD
    T = suffix_kv.shape[1]
    W = out_weight.shape[1]
    R = residual.shape[0]
    RC = R // C
    VM = pltpu.VMEM
    DMA = pltpu.SemaphoreType.DMA
    n_f = Y // X
    args = (
        queries, new_kv, prefix_kv, suffix_kv,
        (parents * PACK + suffix_len).reshape(G, B),
        out_weight.T, residual.T, steer_dict.T, steer_ids.T, steer_strength.T,
        norm_gain[None], norm_bias[None],
    )
    in_hbm = (1, 2, 3, 5, 7)
    big = max(NX, Z)
    scratch = (
        [VM((S, split), BF16)] * 4
        + [VM((S, wide), BF16)] * 4
        + [VM((S, split + HEAD), BF16)] * 4
        + [VM((S, wide + HEAD), BF16)] * 4
        + [
            VM(new_kv.shape, BF16), VM(prefix_kv.shape, BF16), VM(suffix_kv.shape, BF16),
            VM((B * T, width), BF16), VM((B * T, width), BF16), VM(steer_dict.T.shape, BF16),
            VM((B, width), F32), VM((heads2, B, HEAD), F32), VM((heads2, B, HEAD), F32),
            VM((B, split), BF16), VM((B, wide), BF16),
            VM((X, Z // n_f, n_f, B, split), BF16), VM((X, Z // n_f, n_f, B, wide), BF16),
            VM((Y, C, W, width), BF16),
            VM((W, R), F32), VM((C * W, RC), F32), VM((W, RC), F32),
            VM((8, R), F32), VM((8, R), F32), VM((NX, 8, R), F32), VM((Z, 8, R), F32),
        ]
        + [DMA((8, big))] * 2
        + [DMA((2, big))] * 2
        + [DMA((2, Y // 2))] * 2
        + [DMA((Y,))] * 2
        + [DMA((2, Z // 2))] * 2
        + [DMA((Z, 2, X // 2))] * 2
        + [DMA((2, X // 2))] * 2
        + [DMA((X, 2, Z // 2))] * 2
        + [DMA((2,))] * 2
        + [DMA((5,)), DMA, DMA]
    )
    out = pl.pallas_call(
        functools.partial(kernel, Y),
        out_shape=jax.ShapeDtypeStruct((W, R), BF16),
        in_specs=[pl.BlockSpec(memory_space=pl.ANY if i in in_hbm else VM) for i in range(len(args))],
        out_specs=pl.BlockSpec(memory_space=VM),
        scratch_shapes=scratch,
        compiler_params=pltpu.CompilerParams(
            collective_id=0, has_side_effects=True, vmem_limit_bytes=56 * 1024 * 1024
        ),
        name="beam_step",
    )(*args)
    return out.T


def solution(mesh):
    placed = (
        P("dp", "tensor"),
        P("dp", None, "tensor"),
        P(None, None, "tensor"),
        P("dp", None, None, "tensor"),
        P(),
        P(),
        P("tensor", "dp"),
        P("tensor", "dp"),
        P(None, "dp"),
        P("tensor", None),
        P("tensor", None),
        P("dp"),
        P("dp"),
    )
    return jax.shard_map(
        on_device, mesh=mesh, in_specs=placed, out_specs=P("tensor", "dp"), check_vma=False
    )
```

```python
import functools

import jax
import jax.numpy as jnp
from jax import lax
from jax.experimental import pallas as pl
from jax.experimental.pallas import tpu as pltpu
from jax.sharding import PartitionSpec as P

MESH = pl.DeviceIdType.MESH
F32, BF16, I32 = jnp.float32, jnp.bfloat16, jnp.int32
D = 10240
HEAD = 128
CAP = 2
PACK = 16
X, Z, C = 4, 8, 2

NEG = -1e30
NT = (((1,), (1,)), ((), ()))
TN = (((0,), (0,)), ((), ()))


def iota(shape, dim):
    return lax.broadcasted_iota(I32, shape, dim)


def log2(n):
    return n.bit_length() - 1


def dot(a, b, dims=(((1,), (0,)), ((), ()))):
    return lax.dot_general(a, b, dims, preferred_element_type=F32)


def rows(start, size):
    return pl.ds(pl.multiple_of(start, size & -size), size)


def heads_of(width):
    heads = width // HEAD
    first = max(1, heads * 3 // 5)
    return first * HEAD, first, heads - first


class Exchange:
    def __init__(self, src, dst, n, me, peer_id, send, recv, chunk, chunk_of=lambda i: i):
        self.src, self.dst, self.n, self.me = src, dst, n, me
        self.peer_id, self.send, self.recv, self.chunk = peer_id, send, recv, chunk
        self.chunk_of = chunk_of

    def copy(self, k, to, out_at, in_at):
        return pltpu.make_async_remote_copy(
            src_ref=self.src.at[rows(out_at * self.chunk, self.chunk)],
            dst_ref=self.dst.at[rows(in_at * self.chunk, self.chunk)],
            send_sem=self.send.at[k],
            recv_sem=self.recv.at[k],
            device_id=self.peer_id(to),
            device_id_type=MESH,
        )

    def start(self):
        n, me = self.n, self.me

        def step(k, _):
            to = lax.rem(me + k, n)
            self.copy(k, to, self.chunk_of(to), me).start()
            return 0

        lax.fori_loop(1, n, step, 0)
        mine = self.src[rows(self.chunk_of(me) * self.chunk, self.chunk)]
        self.dst[rows(me * self.chunk, self.chunk)] = mine

    def wait(self):
        n, me = self.n, self.me

        def step(k, _):
            frm = lax.rem(me + n - k, n)
            self.copy(k, frm, frm, frm).wait_recv()
            return 0

        lax.fori_loop(1, n, step, 0)

    def drain(self):
        n, me = self.n, self.me

        def step(k, _):
            to = lax.rem(me + k, n)
            self.copy(k, to, self.chunk_of(to), me).wait_send()
            return 0

        lax.fori_loop(1, n, step, 0)


class Share(Exchange):
    def copy(self, k, to, out_at, in_at):
        return pltpu.make_async_remote_copy(
            src_ref=self.src,
            dst_ref=self.dst.at[in_at],
            send_sem=self.send.at[k],
            recv_sem=self.recv.at[k],
            device_id=self.peer_id(to),
            device_id_type=MESH,
        )

    def start(self):
        n, me = self.n, self.me

        def step(k, _):
            to = lax.rem(me + k, n)
            self.copy(k, to, to, me).start()
            return 0

        lax.fori_loop(1, n, step, 0)
        self.dst[me] = self.src[...]


class Ring:
    def __init__(self, view, n, me, peer_id, send, recv, split=False, last_way=0):
        self.view, self.n, self.me, self.peer_id = view, n, me, peer_id
        self.send, self.recv, self.split, self.last_way = send, recv, split, last_way
        self.steps = n // 2

    def moves(self, s):
        if s < 1 or s > self.steps:
            return []
        if 2 * s < self.n:
            return [(0, None), (1, None)]
        return [(0, 0), (1, 1)] if self.split else [(self.last_way, None)]

    def copy(self, s, way, part, index):
        ref = self.view(index, part)
        to = lax.rem(self.me + 1, self.n) if way == 0 else lax.rem(self.me + self.n - 1, self.n)
        return pltpu.make_async_remote_copy(
            src_ref=ref,
            dst_ref=ref,
            send_sem=self.send.at[way, s - 1],
            recv_sem=self.recv.at[way, s - 1],
            device_id=self.peer_id(to),
            device_id_type=MESH,
        )

    def at(self, offset):
        return lax.rem(self.me + offset + self.n, self.n)

    def outgoing(self, s):
        for way, part in self.moves(s):
            yield self.copy(s, way, part, self.at(1 - s if way == 0 else s - 1))

    def start(self, s):
        for c in self.outgoing(s):
            c.start()

    def wait(self, s):
        for way, part in self.moves(s):
            self.copy(s, way, part, self.at(-s if way == 0 else s)).wait_recv()

    def drain(self):
        for s in range(1, self.steps + 1):
            for c in self.outgoing(s):
                c.wait_send()


def three_terms(value):
    top = value.astype(BF16).astype(F32)
    rest = value - top
    middle = rest.astype(BF16).astype(F32)
    return top, middle, rest - middle


def kernel(
    Y,
    q_ref, new_hbm, pre_hbm, suf_hbm, par_ref,
    w_hbm, res_ref, dict_hbm, ids_ref, str_ref, gain_ref, bias_ref,
    out_ref,
    qs_a, q1_a, q2_a, q3_a, qs_b, q1_b, q2_b, q3_b,
    rs_a, r1_a, r2_a, r3_a, rs_b, r1_b, r2_b, r3_b,
    q_guest, new_raw, pre_raw, suf_raw, sk_ref, sv_ref, dict_ref,
    num, top1, den1, att_a, att_b, ag_a, ag_b, wbuf, base, acc, sib, st1, st2, g1, g2,
    ex_send, ex_recv, sh_send, sh_recv, y_send, y_recv, ws_send, ws_recv,
    az_send, az_recv, ax_send, ax_recv, bx_send, bx_recv, bz_send, bz_recv,
    pm_send, pm_recv, in_sem, sb_send, sb_recv,
):
    NX = X * C
    G = NX * Z
    S = G * CAP
    B, width = q_ref.shape
    split, heads_a, heads_b = heads_of(width)
    wide = width - split
    n_a = X * Z // Y
    n_f = Z // n_a
    W = w_hbm.shape[0]
    R = res_ref.shape[1]
    RC = R // C
    scale = HEAD ** (-0.5)

    d = lax.axis_index("dp")
    y = lax.axis_index("tensor")
    c = lax.rem(d, C)
    p = lax.div(d, C)
    z = lax.rem(p, Z)
    x = lax.div(p, Z)
    xc = x * C + c

    def xc_id(i):
        return ((lax.div(i, C) * Z + z) * C + lax.rem(i, C), y)

    def z_id(i):
        return ((x * Z + i) * C + c, y)

    def x_id(i):
        return ((i * Z + z) * C + c, y)

    def y_id(i):
        return (d, i)

    sibling = (p * C + (1 - c), y)
    shift = (Z - n_a) // 2 // n_f * n_f

    def x_guest(i):
        return lax.rem(i - lax.div(y, n_f) + X, X)

    def z_guest(i):
        bit = lax.rem(i, n_f)
        low = lax.rem(bit - y + Y, n_f) * n_a
        return low + lax.div(lax.rem(i - bit - low + shift + Z, Z), n_f)

    z_half = lax.rem(lax.div(p, n_a), n_f)
    x_host = lax.rem(x + lax.div(y, n_f), X)
    z_host = lax.rem(
        z_half * n_a + n_f * lax.rem(z, n_a) - shift + lax.rem(y + z_half, n_f) + Z, Z
    )
    host = ((x_host * Z + z_host) * C + c, y)
    p_guest = x_guest(x) * Z + z_guest(z)
    d_guest = p_guest * C + c
    at_home = d_guest == d
    t_guest = lax.div(p_guest, n_a)

    def y_of(xi, bit):
        return n_f * lax.rem(xi - lax.div(y, n_f) + X, X) + lax.rem(bit - y + Y, n_f)

    y_from = y_of(x, lax.rem(z, n_f))
    in_plane = t_guest == y

    barrier = pltpu.get_barrier_semaphore()

    def hello(dev):
        pl.semaphore_signal(barrier, inc=1, device_id=dev, device_id_type=MESH)

    def greet(peer_id, n, me):
        def step(k, _):
            hello(peer_id(lax.rem(me + k, n)))
            return 0

        lax.fori_loop(1, n, step, 0)

    greet(xc_id, NX, xc)
    greet(z_id, Z, z)
    hello(y_id(lax.rem(y + 1, Y)))
    hello(y_id(lax.rem(y + Y - 1, Y)))


    @pl.when(jnp.logical_not(at_home))
    def _():
        hello((d_guest, y))

    @pl.when(jnp.logical_not(in_plane))
    def _():
        hello(y_id(y_from))

    loads = [
        pltpu.make_async_copy(a, b, in_sem.at[i])
        for i, (a, b) in enumerate((
            (w_hbm, wbuf.at[y, c]), (pre_hbm, pre_raw),
            (suf_hbm, suf_raw), (dict_hbm, dict_ref),
        ))
    ]
    for load in loads:
        load.start()

    r_bits = log2(CAP)
    slot = iota((S, 1), 0)
    rank_of = (slot & (CAP - 1)).astype(F32)
    group = slot >> r_bits
    xc_a, z_a = group >> log2(Z), group & (Z - 1)
    z_b, xc_b = group >> log2(NX), group & (NX - 1)

    def d_of(xc_, z_):
        return (((xc_ >> log2(C)) * Z + z_) * C + (xc_ & (C - 1))).astype(F32)

    d_a, d_b = d_of(xc_a, z_a), d_of(xc_b, z_b)
    before = (iota((B, B), 0) < iota((B, B), 1)).astype(BF16)

    def split_parents(par):
        par = par.astype(F32)
        both = jnp.floor(par * (1.0 / PACK))
        src = jnp.floor((both + 0.5) * (1.0 / B))
        return src, both - src * B, par - both * PACK

    def slots_of(block_src, dest):
        hit = block_src == dest
        rank = dot(hit.astype(BF16), before)
        return (hit & (rank == rank_of)).astype(BF16)

    my_src, _, my_len = split_parents(par_ref[pl.ds(d, 1), :])
    e_a, e_b = slots_of(my_src, d_a), slots_of(my_src, d_b)
    qs_a[...] = dot(e_a, q_ref[:, :split]).astype(BF16)
    qs_b[...] = dot(e_b, q_ref[:, split:]).astype(BF16)

    pl.semaphore_wait(
        barrier, NX - 1 + Z - 1 + 2 + jnp.where(at_home, 0, 1) + jnp.where(in_plane, 0, 1)
    )

    exchanges = []

    def exchange(src, dst, over_z, index, chunk, chunk_of=lambda i: i):
        n, me, peer = (Z, z, z_id) if over_z else (NX, xc, xc_id)
        e = Exchange(src, dst, n, me, peer, ex_send.at[index], ex_recv.at[index], chunk, chunk_of)
        exchanges.append(e)
        return e

    def xc_guest(i):
        return x_guest(lax.div(i, C)) * C + lax.rem(i, C)

    ca, cb = Z * CAP, NX * CAP
    e1a = exchange(qs_a, q1_a, False, 0, ca)
    e1b = exchange(qs_b, q1_b, True, 1, cb)
    e2a = exchange(q2_a, q3_a, True, 2, cb)
    e2b = exchange(q2_b, q3_b, False, 3, ca)
    e3a = exchange(rs_a, r1_a, True, 4, cb, z_guest)
    e3b = exchange(rs_b, r1_b, False, 5, ca, xc_guest)
    e4a = exchange(r2_a, r3_a, False, 6, ca, xc_guest)
    e4b = exchange(r2_b, r3_b, True, 7, cb, z_guest)

    e1a.start()
    e1b.start()

    def lodge(i, src, dst, home):
        if home:
            return pltpu.make_async_copy(src, dst, in_sem.at[4 + i])
        return pltpu.make_async_remote_copy(
            src_ref=src, dst_ref=dst, send_sem=pm_send.at[2 + i], recv_sem=pm_recv.at[2 + i],
            device_id=host, device_id_type=MESH,
        )

    guests = ((q_ref, q_guest), (new_hbm, new_raw))

    @pl.when(at_home)
    def _():
        for i, (src, dst) in enumerate(guests):
            lodge(i, src, dst, True).start()

    @pl.when(jnp.logical_not(at_home))
    def _():
        for i, (src, dst) in enumerate(guests):
            lodge(i, src, dst, False).start()

    def w_block(i, part):
        if part is None:
            return wbuf.at[i, c]
        return wbuf.at[i, c, pl.ds(part * (W // 2), W // 2)]

    loads[0].wait()
    wring = Ring(w_block, Y, y, y_id, y_send, y_recv, True)

    def to_sibling(index, at, core):
        ref = wbuf.at[index, core]
        return pltpu.make_async_remote_copy(
            src_ref=ref, dst_ref=ref, send_sem=ws_send.at[at], recv_sem=ws_recv.at[at],
            device_id=sibling, device_id_type=MESH,
        )

    handed = []

    def hand(offset):
        index = lax.rem(y + offset + Y, Y)
        at = len(handed)
        to_sibling(index, at, c).start()
        handed.append(index)

    wring.start(1)
    hand(0)

    def w_step(s):
        wring.wait(s)
        if s < wring.steps:
            wring.start(s + 1)
        hand(-s)
        if 2 * s < Y:
            hand(s)

    keys = sk_ref.shape[0]
    loads[2].wait()
    for h in range(heads_a + heads_b):
        cols = slice(h * HEAD, (h + 1) * HEAD)
        pair = suf_raw[:, :, :, cols].astype(F32)
        sk_ref[:, cols] = pair[:, :, 0].reshape(keys, HEAD).astype(BF16)
        sv_ref[:, cols] = pair[:, :, 1].reshape(keys, HEAD).astype(BF16)

    out_i, in_j = iota((S, S), 0), iota((S, S), 1)

    def swap(n_out, n_in):
        g = out_i >> r_bits
        u, v = g >> log2(n_in), g & (n_in - 1)
        return (in_j == ((v * n_out + u) * CAP + (out_i & (CAP - 1)))).astype(BF16)

    to_b, to_a = swap(Z, NX), swap(NX, Z)

    e1a.wait()
    q2_a[...] = dot(to_b, q1_a[...]).astype(BF16)
    e2a.start()
    e1b.wait()
    q2_b[...] = dot(to_a, q1_b[...]).astype(BF16)
    e2b.start()

    src, off, _ = split_parents(par_ref[...])
    group_of = iota((S, G), 1).astype(F32)
    T = keys // B
    beam_of = iota((B, keys), 1) >> log2(T)
    spread = (beam_of == iota((B, keys), 0)).astype(BF16)
    live = dot(my_len.astype(BF16), spread)
    live_cols = (iota((1, keys), 1) & (T - 1)).astype(F32) < live
    col_beam = (iota((1, keys), 1) >> log2(T)).astype(F32)
    here = d.astype(F32)

    def mask_of(dest):
        pick = (group_of == dest).astype(BF16)
        hit = dot(pick, src.astype(BF16)) == here
        rank = dot(hit.astype(BF16), before)
        chosen = (hit & (rank == rank_of)).astype(F32)
        offset = jnp.sum(chosen * dot(pick, off.astype(BF16)), axis=1, keepdims=True)
        there = jnp.sum(chosen, axis=1, keepdims=True) > 0.0
        offset = jnp.where(there, offset, -1.0)
        return (offset == col_beam) & live_cols

    feats = dict_ref.shape[1]
    step_f = min(feats, 128)
    base[...] = res_ref[...].astype(F32)
    loads[3].wait()

    def steer(i, _):
        at = i * step_f
        feature = iota((step_f, R), 0) + at
        s = jnp.zeros((step_f, R), F32)
        for k in range(ids_ref.shape[0]):
            s = s + jnp.where(feature == ids_ref[k : k + 1, :], str_ref[k : k + 1, :], 0.0)
        top, middle, _ = three_terms(s)
        part = dict_ref[:, rows(at, step_f)]
        base[...] += dot(part, top.astype(BF16)) + dot(part, middle.astype(BF16))
        return 0

    lax.fori_loop(0, feats // step_f, steer, 0)

    def attend(q3, mask, rs, first, heads):
        lane = iota((S, HEAD), 1)
        extra = jnp.zeros((S, HEAD), F32)
        for i in range(heads):
            cols = slice((first + i) * HEAD, (first + i + 1) * HEAD)
            mine = slice(i * HEAD, (i + 1) * HEAD)
            s = dot(q3[:, mine], sk_ref[:, cols], NT) * scale
            s = jnp.where(mask, s, NEG)
            m = jnp.max(s, axis=1, keepdims=True)
            e = jnp.where(mask, jnp.exp(s - m), 0.0)
            l = jnp.maximum(jnp.sum(e, axis=1, keepdims=True), 1e-30)
            o = dot(e.astype(BF16), sv_ref[:, cols]) / l
            rs[:, mine] = o.astype(BF16)
            for k, term in enumerate(three_terms(m + jnp.log(l))):
                extra = jnp.where(lane == k * heads + i, term, extra)
        rs[:, heads * HEAD :] = extra.astype(BF16)

    mask_b, mask_a = mask_of(d_b), mask_of(d_a)

    loads[1].wait()

    @pl.when(at_home)
    def _():
        for i, (src, dst) in enumerate(guests):
            lodge(i, src, dst, True).wait()

    @pl.when(jnp.logical_not(at_home))
    def _():
        for i, (src, dst) in enumerate(guests):
            lodge(i, src, dst, False).wait_recv()

    for h in range(heads_a + heads_b):
        cols = slice(h * HEAD, (h + 1) * HEAD)
        qh = q_guest[:, cols]
        pre = pre_raw[:, :, cols].astype(F32)
        new = new_raw[:, :, cols].astype(F32)
        s_pre = dot(qh, pre[:, 0].astype(BF16), NT) * scale
        m_pre = jnp.max(s_pre, axis=1, keepdims=True)
        e_pre = jnp.exp(s_pre - m_pre)
        l_pre = jnp.sum(e_pre, axis=1, keepdims=True)
        o_pre = dot(e_pre.astype(BF16), pre[:, 1].astype(BF16))
        s_self = scale * jnp.sum(qh.astype(F32) * new[:, 0], axis=1, keepdims=True)
        m1 = jnp.maximum(m_pre, s_self)
        up, us = jnp.exp(m_pre - m1), jnp.exp(s_self - m1)
        num[:, cols] = up * o_pre + us * new[:, 1]
        top1[h] = jnp.broadcast_to(m1, (B, HEAD))
        den1[h] = jnp.broadcast_to(up * l_pre + us, (B, HEAD))

    w_step(1)
    e2a.wait()
    attend(q3_a, mask_b, rs_a, 0, heads_a)
    e3a.start()
    e2b.wait()
    attend(q3_b, mask_a, rs_b, heads_a, heads_b)
    e3b.start()

    e3a.wait()
    r2_a[...] = dot(to_a, r1_a[...]).astype(BF16)
    e4a.start()
    e3b.wait()
    r2_b[...] = dot(to_b, r1_b[...]).astype(BF16)
    e4b.start()
    if wring.steps > 1:
        w_step(2)

    def merge(e, r3, att, first, heads):
        got = dot(e, r3[...], TN)
        for i in range(heads):
            h = first + i
            mine = slice(i * HEAD, (i + 1) * HEAD)
            extra = heads * HEAD + i
            lse = sum(got[:, extra + k * heads : extra + k * heads + 1] for k in range(3))
            m1 = top1[h]
            m = jnp.maximum(m1, lse)
            a, b = jnp.exp(m1 - m), jnp.exp(lse - m)
            total = a * num[:, h * HEAD : (h + 1) * HEAD] + b * got[:, mine]
            att[:, mine] = (total / (a * den1[h] + b)).astype(BF16)

    def block_a(xi, zi):
        return ag_a.at[xi, lax.div(zi, n_f), lax.rem(zi, n_f)]

    def block_b(xi, zi):
        return ag_b.at[xi, lax.div(zi, n_f), lax.rem(zi, n_f)]

    def place(att, block, at):
        return pltpu.make_async_remote_copy(
            src_ref=att, dst_ref=block(x, z),
            send_sem=pm_send.at[at], recv_sem=pm_recv.at[at],
            device_id=y_id(t_guest), device_id_type=MESH,
        )

    def move(att, block, at):
        @pl.when(in_plane)
        def _():
            block(x, z)[...] = att[...]

        @pl.when(jnp.logical_not(in_plane))
        def _():
            place(att, block, at).start()

    def settle(att, block, at):
        @pl.when(jnp.logical_not(in_plane))
        def _():
            place(att, block, at).wait_recv()

    guest_src, _, _ = split_parents(par_ref[pl.ds(d_guest, 1), :])
    f_a, f_b = slots_of(guest_src, d_a), slots_of(guest_src, d_b)
    e4a.wait()
    merge(f_a, r3_a, att_a, 0, heads_a)
    move(att_a, block_a, 0)
    e4b.wait()
    merge(f_b, r3_b, att_b, heads_a, heads_b)
    move(att_b, block_b, 1)
    if wring.steps > 2:
        w_step(3)

    class Spread:
        def __init__(self, along, across):
            self.along, self.across = along, across

        def round(self, r):
            if r:
                self.along.wait(r)
            self.along.start(r + 1)
            fresh = [0] if r == 0 else [-r, r][: 1 if 2 * r == self.along.n else 2]
            if r <= self.along.steps:
                for o in fresh:
                    self.across[o].start(1)
            for o, ring in self.across.items():
                step = r - abs(o)
                if step > 0:
                    ring.wait(step)
                    ring.start(step + 1)

        def drain(self):
            self.along.drain()
            for ring in self.across.values():
                ring.drain()

    def offsets(n):
        return [0] + [o for k in range(1, n // 2 + 1) for o in ([-k, k] if 2 * k < n else [-k])]

    spread_a = Spread(
        Ring(lambda i, part: block_a(x, i), Z, z, z_id, az_send, az_recv),
        {
            o: Ring(
                lambda i, part, o=o: block_a(i, lax.rem(z + o + Z, Z)),
                X, x, x_id, ax_send.at[k], ax_recv.at[k], last_way=k % 2,
            )
            for k, o in enumerate(offsets(Z))
        },
    )
    spread_b = Spread(
        Ring(lambda i, part: block_b(i, z), X, x, x_id, bx_send, bx_recv),
        {
            o: Ring(
                lambda i, part, o=o: block_b(lax.rem(x + o + X, X), i),
                Z, z, z_id, bz_send.at[k], bz_recv.at[k], last_way=1 - k % 2,
            )
            for k, o in enumerate(offsets(X))
        },
    )
    rounds = (X + Z) // 2

    def multiply(xi, first):
        for bit in range(n_f):
            ys = y_of(xi, bit)
            for ag, at, size in ((ag_a, 0, split), (ag_b, split, wide)):
                weights = wbuf[ys, :, :, at : at + size].reshape(C * W, size)
                part = dot(weights, ag[xi, :, bit].reshape(n_a * B, size), NT)
                if first and bit == 0 and at == 0:
                    acc[...] = part
                else:
                    acc[...] += part

    def weights_here():
        for at, index in enumerate(handed):
            to_sibling(index, at, 1 - c).wait_recv()

    for r in range(rounds + 1):
        if r == 0:
            settle(att_a, block_a, 0)
        spread_a.round(r)
        if r == 0:
            settle(att_b, block_b, 1)
        spread_b.round(r)
        if r == 0 and wring.steps > 3:
            w_step(4)
        if r == Z // 2:
            weights_here()
        if r >= Z // 2:
            k = r - Z // 2
            multiply(lax.rem(x + k, X), k == 0)
            if 0 < 2 * k < X:
                multiply(lax.rem(x + X - k, X), False)

    swap_out = pltpu.make_async_remote_copy(
        src_ref=acc.at[rows((1 - c) * W, W)], dst_ref=sib,
        send_sem=sb_send, recv_sem=sb_recv, device_id=sibling, device_id_type=MESH,
    )
    swap_out.start()
    ri, ci = iota((RC, R), 0), iota((RC, R), 1)
    turn = n_a - lax.rem(y, n_f) * (n_a // n_f) + shift // n_f
    block_no = sum((ri >= B * k).astype(I32) for k in range(1, n_a))
    inner = ri - block_no * B
    place_no = (block_no + turn) & (n_a - 1)

    def spot(cls):
        return (ci == (place_no * C + cls) * B + inner).astype(F32)

    def put(value, cls):
        return lax.dot_general(
            value, spot(cls), (((1,), (0,)), ((), ())),
            preferred_element_type=F32, precision=lax.Precision.HIGHEST,
        )

    summed = base[...] + put(acc[rows(c * W, W), :], c)
    swap_out.wait_recv()
    summed = summed + put(sib[...], 1 - c)

    def join(got, n_each):
        n = got.shape[0]
        means, squares = got[:, 0:1, :], got[:, 1:2, :]
        mean = jnp.sum(means, axis=0) * (1.0 / n)
        away = means - mean[None]
        square = jnp.sum(squares, axis=0) + n_each * jnp.sum(away * away, axis=0)
        return mean, square

    row_no = iota((8, R), 0)

    def pack(mean, square):
        return jnp.where(row_no == 0, mean, jnp.where(row_no == 1, square, 0.0))

    mean = jnp.sum(summed, axis=0, keepdims=True) * (1.0 / W)
    away = summed - mean
    st1[...] = pack(mean, jnp.sum(away * away, axis=0, keepdims=True))
    s1 = Share(st1, g1, NX, xc, xc_id, sh_send.at[0], sh_recv.at[0], 1)
    s1.start()
    eye = iota((W, W), 0) == iota((W, W), 1)
    gain = jnp.sum(jnp.where(eye, gain_ref[...], 0.0), axis=1, keepdims=True)
    bias = jnp.sum(jnp.where(eye, bias_ref[...], 0.0), axis=1, keepdims=True)
    s1.wait()
    st2[...] = pack(*join(g1[...], float(W)))
    s2 = Share(st2, g2, Z, z, z_id, sh_send.at[1], sh_recv.at[1], 1)
    s2.start()
    s2.wait()
    mean, square = join(g2[...], float(W * NX))
    var = square * (1.0 / (W * NX * Z))
    normed = (summed - mean) * lax.rsqrt(var + 1e-5)
    out_ref[...] = (normed * gain + bias).astype(BF16)

    for e in exchanges:
        e.drain()
    s1.drain()
    s2.drain()
    for ring in (wring, spread_a, spread_b):
        ring.drain()

    @pl.when(jnp.logical_not(in_plane))
    def _():
        place(att_a, block_a, 0).wait_send()
        place(att_b, block_b, 1).wait_send()

    @pl.when(jnp.logical_not(at_home))
    def _():
        for i, (src, dst) in enumerate(guests):
            lodge(i, src, dst, False).wait_send()

    for at, index in enumerate(handed):
        to_sibling(index, at, c).wait_send()
    swap_out.wait_send()


def on_device(
    queries, new_kv, prefix_kv, suffix_kv, suffix_len, parents, out_weight, residual,
    steer_dict, steer_ids, steer_strength, norm_gain, norm_bias,
):
    G = lax.axis_size("dp")
    Y = lax.axis_size("tensor")
    NX = X * C
    S = G * CAP
    B, width = queries.shape
    split, heads_a, heads_b = heads_of(width)
    wide = width - split
    heads2 = width // HEAD
    T = suffix_kv.shape[1]
    W = out_weight.shape[1]
    R = residual.shape[0]
    RC = R // C
    VM = pltpu.VMEM
    DMA = pltpu.SemaphoreType.DMA
    n_f = Y // X
    args = (
        queries, new_kv, prefix_kv, suffix_kv,
        (parents * PACK + suffix_len).reshape(G, B),
        out_weight.T, residual.T, steer_dict.T, steer_ids.T, steer_strength.T,
        norm_gain[None], norm_bias[None],
    )
    in_hbm = (1, 2, 3, 5, 7)
    big = max(NX, Z)
    scratch = (
        [VM((S, split), BF16)] * 4
        + [VM((S, wide), BF16)] * 4
        + [VM((S, split + HEAD), BF16)] * 4
        + [VM((S, wide + HEAD), BF16)] * 4
        + [
            VM((B, width), BF16), VM(new_kv.shape, BF16), VM(prefix_kv.shape, BF16), VM(suffix_kv.shape, BF16),
            VM((B * T, width), BF16), VM((B * T, width), BF16), VM(steer_dict.T.shape, BF16),
            VM((B, width), F32), VM((heads2, B, HEAD), F32), VM((heads2, B, HEAD), F32),
            VM((B, split), BF16), VM((B, wide), BF16),
            VM((X, Z // n_f, n_f, B, split), BF16), VM((X, Z // n_f, n_f, B, wide), BF16),
            VM((Y, C, W, width), BF16),
            VM((W, R), F32), VM((C * W, RC), F32), VM((W, RC), F32),
            VM((8, R), F32), VM((8, R), F32), VM((NX, 8, R), F32), VM((Z, 8, R), F32),
        ]
        + [DMA((8, big))] * 2
        + [DMA((2, big))] * 2
        + [DMA((2, Y // 2))] * 2
        + [DMA((Y,))] * 2
        + [DMA((2, Z // 2))] * 2
        + [DMA((Z, 2, X // 2))] * 2
        + [DMA((2, X // 2))] * 2
        + [DMA((X, 2, Z // 2))] * 2
        + [DMA((4,))] * 2
        + [DMA((6,)), DMA, DMA]
    )
    out = pl.pallas_call(
        functools.partial(kernel, Y),
        out_shape=jax.ShapeDtypeStruct((W, R), BF16),
        in_specs=[pl.BlockSpec(memory_space=pl.ANY if i in in_hbm else VM) for i in range(len(args))],
        out_specs=pl.BlockSpec(memory_space=VM),
        scratch_shapes=scratch,
        compiler_params=pltpu.CompilerParams(
            collective_id=0, has_side_effects=True, vmem_limit_bytes=56 * 1024 * 1024
        ),
        name="beam_step",
    )(*args)
    return out.T


def solution(mesh):
    placed = (
        P("dp", "tensor"),
        P("dp", None, "tensor"),
        P(None, None, "tensor"),
        P("dp", None, None, "tensor"),
        P(),
        P(),
        P("tensor", "dp"),
        P("tensor", "dp"),
        P(None, "dp"),
        P("tensor", None),
        P("tensor", None),
        P("dp"),
        P("dp"),
    )
    return jax.shard_map(
        on_device, mesh=mesh, in_specs=placed, out_specs=P("tensor", "dp"), check_vma=False
    )
```

```python
import functools
import itertools

import jax
import jax.numpy as jnp
from jax import lax
from jax.experimental import pallas as pl
from jax.experimental.pallas import tpu as pltpu
from jax.sharding import PartitionSpec as P

MESH = pl.DeviceIdType.MESH
F32, BF16, I32 = jnp.float32, jnp.bfloat16, jnp.int32
D = 10240
HEAD = 128
CAP = 2
PACK = 16
X, Z, C = 4, 8, 2

NEG = -1e30
NT = (((1,), (1,)), ((), ()))
TN = (((0,), (0,)), ((), ()))


def iota(shape, dim):
    return lax.broadcasted_iota(I32, shape, dim)


def log2(n):
    return n.bit_length() - 1


def dot(a, b, dims=(((1,), (0,)), ((), ()))):
    return lax.dot_general(a, b, dims, preferred_element_type=F32)


def rows(start, size):
    return pl.ds(pl.multiple_of(start, size & -size), size)


def heads_of(width):
    heads = width // HEAD
    first = max(1, heads * 3 // 5)
    return first * HEAD, first, heads - first


class Exchange:
    def __init__(self, src, dst, n, me, peer_id, send, recv, chunk, chunk_of=lambda i: i):
        self.src, self.dst, self.n, self.me = src, dst, n, me
        self.peer_id, self.send, self.recv, self.chunk = peer_id, send, recv, chunk
        self.chunk_of = chunk_of

    def copy(self, k, to, out_at, in_at):
        return pltpu.make_async_remote_copy(
            src_ref=self.src.at[rows(out_at * self.chunk, self.chunk)],
            dst_ref=self.dst.at[rows(in_at * self.chunk, self.chunk)],
            send_sem=self.send.at[k],
            recv_sem=self.recv.at[k],
            device_id=self.peer_id(to),
            device_id_type=MESH,
        )

    def start(self):
        n, me = self.n, self.me

        def step(k, _):
            to = lax.rem(me + k, n)
            self.copy(k, to, self.chunk_of(to), me).start()
            return 0

        lax.fori_loop(1, n, step, 0)
        mine = self.src[rows(self.chunk_of(me) * self.chunk, self.chunk)]
        self.dst[rows(me * self.chunk, self.chunk)] = mine

    def wait(self):
        n, me = self.n, self.me

        def step(k, _):
            frm = lax.rem(me + n - k, n)
            self.copy(k, frm, frm, frm).wait_recv()
            return 0

        lax.fori_loop(1, n, step, 0)

    def drain(self):
        n, me = self.n, self.me

        def step(k, _):
            to = lax.rem(me + k, n)
            self.copy(k, to, self.chunk_of(to), me).wait_send()
            return 0

        lax.fori_loop(1, n, step, 0)


class Share(Exchange):
    def copy(self, k, to, out_at, in_at):
        return pltpu.make_async_remote_copy(
            src_ref=self.src,
            dst_ref=self.dst.at[in_at],
            send_sem=self.send.at[k],
            recv_sem=self.recv.at[k],
            device_id=self.peer_id(to),
            device_id_type=MESH,
        )

    def start(self):
        n, me = self.n, self.me

        def step(k, _):
            to = lax.rem(me + k, n)
            self.copy(k, to, to, me).start()
            return 0

        lax.fori_loop(1, n, step, 0)
        self.dst[me] = self.src[...]


class Ring:
    def __init__(self, view, n, me, peer_id, send, recv, split=False, last_way=0):
        self.view, self.n, self.me, self.peer_id = view, n, me, peer_id
        self.send, self.recv, self.split, self.last_way = send, recv, split, last_way
        self.steps = n // 2

    def moves(self, s):
        if s < 1 or s > self.steps:
            return []
        if 2 * s < self.n:
            return [(0, None), (1, None)]
        return [(0, 0), (1, 1)] if self.split else [(self.last_way, None)]

    def copy(self, s, way, part, index):
        ref = self.view(index, part)
        to = lax.rem(self.me + 1, self.n) if way == 0 else lax.rem(self.me + self.n - 1, self.n)
        return pltpu.make_async_remote_copy(
            src_ref=ref,
            dst_ref=ref,
            send_sem=self.send.at[way, s - 1],
            recv_sem=self.recv.at[way, s - 1],
            device_id=self.peer_id(to),
            device_id_type=MESH,
        )

    def at(self, offset):
        return lax.rem(self.me + offset + self.n, self.n)

    def outgoing(self, s):
        for way, part in self.moves(s):
            yield self.copy(s, way, part, self.at(1 - s if way == 0 else s - 1))

    def start(self, s):
        for c in self.outgoing(s):
            c.start()

    def wait(self, s):
        for way, part in self.moves(s):
            self.copy(s, way, part, self.at(-s if way == 0 else s)).wait_recv()

    def drain(self):
        for s in range(1, self.steps + 1):
            for c in self.outgoing(s):
                c.wait_send()


def three_terms(value):
    top = value.astype(BF16).astype(F32)
    rest = value - top
    middle = rest.astype(BF16).astype(F32)
    return top, middle, rest - middle


def kernel(
    Y,
    q_ref, new_hbm, pre_hbm, suf_hbm, par_ref,
    w_hbm, res_ref, dict_hbm, ids_ref, str_ref, gain_ref, bias_ref,
    out_ref,
    qs_a, q1_a, q2_a, q3_a, qs_b, q1_b, q2_b, q3_b,
    rs_a, r1_a, r2_a, r3_a, rs_b, r1_b, r2_b, r3_b,
    q_guest, new_raw, pre_raw, suf_raw, sk_ref, sv_ref, dict_ref,
    num, top1, den1, att_a, att_b, ag_a, ag_b, wbuf, base, base_c, acc, sib, st1, st2, g1, g2,
    ex_send, ex_recv, sh_send, sh_recv, y_send, y_recv, ws_send, ws_recv,
    az_send, az_recv, ax_send, ax_recv, bx_send, bx_recv, bz_send, bz_recv,
    pm_send, pm_recv, in_sem, sb_send, sb_recv,
):
    NX = X * C
    G = NX * Z
    S = G * CAP
    B, width = q_ref.shape
    split, heads_a, heads_b = heads_of(width)
    wide = width - split
    n_a = X * Z // Y
    n_f = Z // n_a
    W = w_hbm.shape[0]
    R = res_ref.shape[1]
    RC = R // C
    scale = HEAD ** (-0.5)

    d = lax.axis_index("dp")
    y = lax.axis_index("tensor")
    c = lax.rem(d, C)
    p = lax.div(d, C)
    z = lax.rem(p, Z)
    x = lax.div(p, Z)
    xc = x * C + c

    def xc_id(i):
        return ((lax.div(i, C) * Z + z) * C + lax.rem(i, C), y)

    def z_id(i):
        return ((x * Z + i) * C + c, y)

    def x_id(i):
        return ((i * Z + z) * C + c, y)

    def y_id(i):
        return (d, i)

    sibling = (p * C + (1 - c), y)
    shift = (Z - n_a) // 2 // n_f * n_f

    def x_guest(i):
        return lax.rem(i - lax.div(y, n_f) + X, X)

    def z_guest(i):
        bit = lax.rem(i, n_f)
        low = lax.rem(bit - y + Y, n_f) * n_a
        return low + lax.div(lax.rem(i - bit - low + shift + Z, Z), n_f)

    z_half = lax.rem(lax.div(p, n_a), n_f)
    x_host = lax.rem(x + lax.div(y, n_f), X)
    z_host = lax.rem(
        z_half * n_a + n_f * lax.rem(z, n_a) - shift + lax.rem(y + z_half, n_f) + Z, Z
    )
    host = ((x_host * Z + z_host) * C + c, y)
    p_guest = x_guest(x) * Z + z_guest(z)
    d_guest = p_guest * C + c
    at_home = d_guest == d
    t_guest = lax.div(p_guest, n_a)

    def y_of(xi, bit):
        return n_f * lax.rem(xi - lax.div(y, n_f) + X, X) + lax.rem(bit - y + Y, n_f)

    y_from = y_of(x, lax.rem(z, n_f))
    in_plane = t_guest == y

    barrier = pltpu.get_barrier_semaphore()

    def hello(dev):
        pl.semaphore_signal(barrier, inc=1, device_id=dev, device_id_type=MESH)

    def greet(peer_id, n, me):
        def step(k, _):
            hello(peer_id(lax.rem(me + k, n)))
            return 0

        lax.fori_loop(1, n, step, 0)

    greet(xc_id, NX, xc)
    greet(z_id, Z, z)
    hello(y_id(lax.rem(y + 1, Y)))
    hello(y_id(lax.rem(y + Y - 1, Y)))


    @pl.when(jnp.logical_not(at_home))
    def _():
        hello((d_guest, y))

    @pl.when(jnp.logical_not(in_plane))
    def _():
        hello(y_id(y_from))

    loads = [
        pltpu.make_async_copy(a, b, in_sem.at[i])
        for i, (a, b) in enumerate((
            (w_hbm, wbuf.at[y, c]), (pre_hbm, pre_raw),
            (suf_hbm, suf_raw), (dict_hbm, dict_ref),
        ))
    ]
    for load in loads:
        load.start()

    r_bits = log2(CAP)
    slot = iota((S, 1), 0)
    rank_of = (slot & (CAP - 1)).astype(F32)
    group = slot >> r_bits
    xc_a, z_a = group >> log2(Z), group & (Z - 1)
    z_b, xc_b = group >> log2(NX), group & (NX - 1)

    def d_of(xc_, z_):
        return (((xc_ >> log2(C)) * Z + z_) * C + (xc_ & (C - 1))).astype(F32)

    d_a, d_b = d_of(xc_a, z_a), d_of(xc_b, z_b)
    before = (iota((B, B), 0) < iota((B, B), 1)).astype(BF16)

    def split_parents(par):
        par = par.astype(F32)
        both = jnp.floor(par * (1.0 / PACK))
        src = jnp.floor((both + 0.5) * (1.0 / B))
        return src, both - src * B, par - both * PACK

    def slots_of(block_src, dest):
        hit = block_src == dest
        rank = dot(hit.astype(BF16), before)
        return (hit & (rank == rank_of)).astype(BF16)

    my_src, _, my_len = split_parents(par_ref[pl.ds(d, 1), :])
    e_a, e_b = slots_of(my_src, d_a), slots_of(my_src, d_b)
    qs_a[...] = dot(e_a, q_ref[:, :split]).astype(BF16)
    qs_b[...] = dot(e_b, q_ref[:, split:]).astype(BF16)

    pl.semaphore_wait(
        barrier, NX - 1 + Z - 1 + 2 + jnp.where(at_home, 0, 1) + jnp.where(in_plane, 0, 1)
    )

    exchanges = []

    def exchange(src, dst, over_z, index, chunk, chunk_of=lambda i: i):
        n, me, peer = (Z, z, z_id) if over_z else (NX, xc, xc_id)
        e = Exchange(src, dst, n, me, peer, ex_send.at[index], ex_recv.at[index], chunk, chunk_of)
        exchanges.append(e)
        return e

    def xc_guest(i):
        return x_guest(lax.div(i, C)) * C + lax.rem(i, C)

    ca, cb = Z * CAP, NX * CAP
    e1a = exchange(qs_a, q1_a, False, 0, ca)
    e1b = exchange(qs_b, q1_b, True, 1, cb)
    e2a = exchange(q2_a, q3_a, True, 2, cb)
    e2b = exchange(q2_b, q3_b, False, 3, ca)
    e3a = exchange(rs_a, r1_a, True, 4, cb, z_guest)
    e3b = exchange(rs_b, r1_b, False, 5, ca, xc_guest)
    e4a = exchange(r2_a, r3_a, False, 6, ca, xc_guest)
    e4b = exchange(r2_b, r3_b, True, 7, cb, z_guest)

    e1a.start()
    e1b.start()

    def lodge(i, src, dst, home):
        if home:
            return pltpu.make_async_copy(src, dst, in_sem.at[4 + i])
        return pltpu.make_async_remote_copy(
            src_ref=src, dst_ref=dst, send_sem=pm_send.at[2 + i], recv_sem=pm_recv.at[2 + i],
            device_id=host, device_id_type=MESH,
        )

    guests = ((q_ref, q_guest), (new_hbm, new_raw))

    def w_block(i, part):
        if part is None:
            return wbuf.at[i, c]
        return wbuf.at[i, c, pl.ds(part * (W // 2), W // 2)]

    loads[0].wait()
    wring = Ring(w_block, Y, y, y_id, y_send, y_recv, True)

    def to_sibling(index, at, core):
        ref = wbuf.at[index, core]
        return pltpu.make_async_remote_copy(
            src_ref=ref, dst_ref=ref, send_sem=ws_send.at[at], recv_sem=ws_recv.at[at],
            device_id=sibling, device_id_type=MESH,
        )

    handed = []

    def hand(offset):
        index = lax.rem(y + offset + Y, Y)
        at = len(handed)
        to_sibling(index, at, c).start()
        handed.append(index)

    wring.start(1)
    hand(0)

    def w_step(s):
        wring.wait(s)
        if s < wring.steps:
            wring.start(s + 1)
        hand(-s)
        if 2 * s < Y:
            hand(s)

    keys = sk_ref.shape[0]
    loads[2].wait()
    for h in range(heads_a + heads_b):
        cols = slice(h * HEAD, (h + 1) * HEAD)
        pair = suf_raw[:, :, :, cols].astype(F32)
        sk_ref[:, cols] = pair[:, :, 0].reshape(keys, HEAD).astype(BF16)
        sv_ref[:, cols] = pair[:, :, 1].reshape(keys, HEAD).astype(BF16)

    out_i, in_j = iota((S, S), 0), iota((S, S), 1)

    def swap(n_out, n_in):
        g = out_i >> r_bits
        u, v = g >> log2(n_in), g & (n_in - 1)
        return (in_j == ((v * n_out + u) * CAP + (out_i & (CAP - 1)))).astype(BF16)

    to_b, to_a = swap(Z, NX), swap(NX, Z)

    e1a.wait()
    q2_a[...] = dot(to_b, q1_a[...]).astype(BF16)
    e2a.start()
    e1b.wait()
    q2_b[...] = dot(to_a, q1_b[...]).astype(BF16)
    e2b.start()

    src, off, _ = split_parents(par_ref[...])
    group_of = iota((S, G), 1).astype(F32)
    T = keys // B
    beam_of = iota((B, keys), 1) >> log2(T)
    spread = (beam_of == iota((B, keys), 0)).astype(BF16)
    live = dot(my_len.astype(BF16), spread)
    live_cols = (iota((1, keys), 1) & (T - 1)).astype(F32) < live
    col_beam = (iota((1, keys), 1) >> log2(T)).astype(F32)
    here = d.astype(F32)

    def mask_of(dest):
        pick = (group_of == dest).astype(BF16)
        hit = dot(pick, src.astype(BF16)) == here
        rank = dot(hit.astype(BF16), before)
        chosen = (hit & (rank == rank_of)).astype(F32)
        offset = jnp.sum(chosen * dot(pick, off.astype(BF16)), axis=1, keepdims=True)
        there = jnp.sum(chosen, axis=1, keepdims=True) > 0.0
        offset = jnp.where(there, offset, -1.0)
        return (offset == col_beam) & live_cols

    feats = dict_ref.shape[1]
    step_f = min(feats, 128)
    base[...] = res_ref[...].astype(F32)
    loads[3].wait()

    def steer(i, _):
        at = i * step_f
        feature = iota((step_f, R), 0) + at
        s = jnp.zeros((step_f, R), F32)
        for k in range(ids_ref.shape[0]):
            s = s + jnp.where(feature == ids_ref[k : k + 1, :], str_ref[k : k + 1, :], 0.0)
        top, middle, _ = three_terms(s)
        part = dict_ref[:, rows(at, step_f)]
        base[...] += dot(part, top.astype(BF16)) + dot(part, middle.astype(BF16))
        return 0

    lax.fori_loop(0, feats // step_f, steer, 0)

    ri, ci = iota((RC, R), 0), iota((RC, R), 1)
    turn = n_a - lax.rem(y, n_f) * (n_a // n_f) + shift // n_f
    block_no = sum((ri >= B * k).astype(I32) for k in range(1, n_a))
    place_no = (block_no + turn) & (n_a - 1)

    def spot(core):
        return (ci == (place_no * C + core) * B + ri - block_no * B).astype(F32)

    for k in range(C):
        base_c[k] = lax.dot_general(
            base[...], spot(k), NT, preferred_element_type=F32, precision=lax.Precision.HIGHEST
        )

    def attend(q3, mask, rs, first, heads):
        lane = iota((S, HEAD), 1)
        extra = jnp.zeros((S, HEAD), F32)
        for i in range(heads):
            cols = slice((first + i) * HEAD, (first + i + 1) * HEAD)
            mine = slice(i * HEAD, (i + 1) * HEAD)
            s = dot(q3[:, mine], sk_ref[:, cols], NT) * scale
            s = jnp.where(mask, s, NEG)
            m = jnp.max(s, axis=1, keepdims=True)
            e = jnp.where(mask, jnp.exp(s - m), 0.0)
            l = jnp.maximum(jnp.sum(e, axis=1, keepdims=True), 1e-30)
            o = dot(e.astype(BF16), sv_ref[:, cols]) / l
            rs[:, mine] = o.astype(BF16)
            for k, term in enumerate(three_terms(m + jnp.log(l))):
                extra = jnp.where(lane == k * heads + i, term, extra)
        rs[:, heads * HEAD :] = extra.astype(BF16)

    mask_b, mask_a = mask_of(d_b), mask_of(d_a)

    w_step(1)
    e2a.wait()
    @pl.when(at_home)
    def _():
        for i, (src, dst) in enumerate(guests):
            lodge(i, src, dst, True).start()

    @pl.when(jnp.logical_not(at_home))
    def _():
        for i, (src, dst) in enumerate(guests):
            lodge(i, src, dst, False).start()

    attend(q3_a, mask_b, rs_a, 0, heads_a)
    e3a.start()
    e2b.wait()
    attend(q3_b, mask_a, rs_b, heads_a, heads_b)
    e3b.start()

    loads[1].wait()

    @pl.when(at_home)
    def _():
        for i, (src, dst) in enumerate(guests):
            lodge(i, src, dst, True).wait()

    @pl.when(jnp.logical_not(at_home))
    def _():
        for i, (src, dst) in enumerate(guests):
            lodge(i, src, dst, False).wait_recv()

    for h in range(heads_a + heads_b):
        cols = slice(h * HEAD, (h + 1) * HEAD)
        qh = q_guest[:, cols]
        pre = pre_raw[:, :, cols].astype(F32)
        new = new_raw[:, :, cols].astype(F32)
        s_pre = dot(qh, pre[:, 0].astype(BF16), NT) * scale
        m_pre = jnp.max(s_pre, axis=1, keepdims=True)
        e_pre = jnp.exp(s_pre - m_pre)
        l_pre = jnp.sum(e_pre, axis=1, keepdims=True)
        o_pre = dot(e_pre.astype(BF16), pre[:, 1].astype(BF16))
        s_self = scale * jnp.sum(qh.astype(F32) * new[:, 0], axis=1, keepdims=True)
        m1 = jnp.maximum(m_pre, s_self)
        up, us = jnp.exp(m_pre - m1), jnp.exp(s_self - m1)
        num[:, cols] = up * o_pre + us * new[:, 1]
        top1[h] = jnp.broadcast_to(m1, (B, HEAD))
        den1[h] = jnp.broadcast_to(up * l_pre + us, (B, HEAD))

    if wring.steps > 1:
        w_step(2)
    e3a.wait()
    r2_a[...] = dot(to_a, r1_a[...]).astype(BF16)
    e4a.start()
    e3b.wait()
    r2_b[...] = dot(to_b, r1_b[...]).astype(BF16)
    e4b.start()
    def merge(e, r3, att, first, heads):
        got = dot(e, r3[...], TN)
        for i in range(heads):
            h = first + i
            mine = slice(i * HEAD, (i + 1) * HEAD)
            extra = heads * HEAD + i
            lse = sum(got[:, extra + k * heads : extra + k * heads + 1] for k in range(3))
            m1 = top1[h]
            m = jnp.maximum(m1, lse)
            a, b = jnp.exp(m1 - m), jnp.exp(lse - m)
            total = a * num[:, h * HEAD : (h + 1) * HEAD] + b * got[:, mine]
            att[:, mine] = (total / (a * den1[h] + b)).astype(BF16)

    def block_a(xi, zi):
        return ag_a.at[xi, lax.div(zi, n_f), lax.rem(zi, n_f)]

    def block_b(xi, zi):
        return ag_b.at[xi, lax.div(zi, n_f), lax.rem(zi, n_f)]

    def place(att, block, at):
        return pltpu.make_async_remote_copy(
            src_ref=att, dst_ref=block(x, z),
            send_sem=pm_send.at[at], recv_sem=pm_recv.at[at],
            device_id=y_id(t_guest), device_id_type=MESH,
        )

    def move(att, block, at):
        @pl.when(in_plane)
        def _():
            block(x, z)[...] = att[...]

        @pl.when(jnp.logical_not(in_plane))
        def _():
            place(att, block, at).start()

    def settle(att, block, at):
        @pl.when(jnp.logical_not(in_plane))
        def _():
            place(att, block, at).wait_recv()

    guest_src, _, _ = split_parents(par_ref[pl.ds(d_guest, 1), :])
    f_a, f_b = slots_of(guest_src, d_a), slots_of(guest_src, d_b)
    e4a.wait()
    merge(f_a, r3_a, att_a, 0, heads_a)
    move(att_a, block_a, 0)
    e4b.wait()
    merge(f_b, r3_b, att_b, heads_a, heads_b)
    move(att_b, block_b, 1)

    class Spread:
        def __init__(self, along, across):
            self.along, self.across = along, across

        def jobs(self, r):
            def source():
                if r:
                    self.along.wait(r)
                self.along.start(r + 1)
                fresh = [0] if r == 0 else [-r, r][: 1 if 2 * r == self.along.n else 2]
                if r <= self.along.steps:
                    for o in fresh:
                        self.across[o].start(1)

            def pass_on(ring, step):
                ring.wait(step)
                ring.start(step + 1)

            yield source
            for o, ring in self.across.items():
                if 0 < r - abs(o) <= ring.steps:
                    yield functools.partial(pass_on, ring, r - abs(o))

        def drain(self):
            self.along.drain()
            for ring in self.across.values():
                ring.drain()

    def offsets(n):
        return [0] + [o for k in range(1, n // 2 + 1) for o in ([-k, k] if 2 * k < n else [-k])]

    spread_a = Spread(
        Ring(lambda i, part: block_a(x, i), Z, z, z_id, az_send, az_recv),
        {
            o: Ring(
                lambda i, part, o=o: block_a(i, lax.rem(z + o + Z, Z)),
                X, x, x_id, ax_send.at[k], ax_recv.at[k], last_way=k % 2,
            )
            for k, o in enumerate(offsets(Z))
        },
    )
    spread_b = Spread(
        Ring(lambda i, part: block_b(i, z), X, x, x_id, bx_send, bx_recv),
        {
            o: Ring(
                lambda i, part, o=o: block_b(lax.rem(x + o + X, X), i),
                Z, z, z_id, bz_send.at[k], bz_recv.at[k], last_way=1 - k % 2,
            )
            for k, o in enumerate(offsets(X))
        },
    )
    rounds = (X + Z) // 2

    def multiply(xi, first):
        for bit in range(n_f):
            ys = y_of(xi, bit)
            for ag, at, size in ((ag_a, 0, split), (ag_b, split, wide)):
                weights = wbuf[ys, :, :, at : at + size].reshape(C * W, size)
                part = dot(weights, ag[xi, :, bit].reshape(n_a * B, size), NT)
                if first and bit == 0 and at == 0:
                    acc[...] = part
                else:
                    acc[...] += part

    def weights_here():
        for at, index in enumerate(handed):
            to_sibling(index, at, 1 - c).wait_recv()

    for r in range(rounds + 1):
        if r == 0:
            settle(att_a, block_a, 0)
        for job_a, job_b in itertools.zip_longest(spread_a.jobs(r), spread_b.jobs(r)):
            if job_a:
                job_a()
            if r == 0 and job_b:
                settle(att_b, block_b, 1)
            if job_b:
                job_b()
        if r == 0 and wring.steps > 2:
            w_step(3)
        if r == Z // 4 and wring.steps > 3:
            w_step(4)
        if r == Z // 2:
            weights_here()
        if r >= Z // 2:
            k = r - Z // 2
            multiply(lax.rem(x + k, X), k == 0)
            if 0 < 2 * k < X:
                multiply(lax.rem(x + X - k, X), False)

    swap_out = pltpu.make_async_remote_copy(
        src_ref=acc.at[rows((1 - c) * W, W)], dst_ref=sib,
        send_sem=sb_send, recv_sem=sb_recv, device_id=sibling, device_id_type=MESH,
    )
    swap_out.start()
    acc[rows(c * W, W), :] += base_c[c]

    def join(got, n_each, core):
        n = got.shape[0]
        means, squares = got[:, 2 * core : 2 * core + 1, :], got[:, 2 * core + 1 : 2 * core + 2, :]
        mean = jnp.sum(means, axis=0) * (1.0 / n)
        away = means - mean[None]
        square = jnp.sum(squares, axis=0) + n_each * jnp.sum(away * away, axis=0)
        return mean, square

    row_no = iota((8, RC), 0)

    def pack(stats, core):
        mean, square = stats
        return jnp.where(row_no == core * 2, mean, jnp.where(row_no == core * 2 + 1, square, 0.0))

    def stats_of(value):
        mean = jnp.sum(value, axis=0, keepdims=True) * (1.0 / W)
        away = value - mean
        return mean, jnp.sum(away * away, axis=0, keepdims=True)

    mine = pack(stats_of(acc[rows(c * W, W), :]), c)
    swap_out.wait_recv()
    sib[...] += base_c[1 - c]
    st1[...] = mine + pack(stats_of(sib[...]), 1 - c)
    s1 = Share(st1, g1, NX, xc, xc_id, sh_send.at[0], sh_recv.at[0], 1)
    s1.start()
    eye = iota((W, W), 0) == iota((W, W), 1)
    gain = jnp.sum(jnp.where(eye, gain_ref[...], 0.0), axis=1, keepdims=True)
    bias = jnp.sum(jnp.where(eye, bias_ref[...], 0.0), axis=1, keepdims=True)
    s1.wait()
    st2[...] = sum(pack(join(g1[...], float(W), k), k) for k in range(C))
    s2 = Share(st2, g2, Z, z, z_id, sh_send.at[1], sh_recv.at[1], 1)
    s2.start()
    s2.wait()
    def normed(value, core):
        mean, square = joined[core]
        var = square * (1.0 / (W * NX * Z))
        return ((value - mean) * lax.rsqrt(var + 1e-5) * gain + bias).astype(BF16)

    joined = [join(g2[...], float(W * NX), k) for k in range(C)]
    own = acc[rows(c * W, W), :]
    parts = [normed(jnp.where(c == k, own, sib[...]), k) for k in range(C)]
    out_ref[...] = sum(dot(part, spot(k).astype(BF16)) for k, part in enumerate(parts)).astype(BF16)

    for e in exchanges:
        e.drain()
    s1.drain()
    s2.drain()
    for ring in (wring, spread_a, spread_b):
        ring.drain()

    @pl.when(jnp.logical_not(in_plane))
    def _():
        place(att_a, block_a, 0).wait_send()
        place(att_b, block_b, 1).wait_send()

    @pl.when(jnp.logical_not(at_home))
    def _():
        for i, (src, dst) in enumerate(guests):
            lodge(i, src, dst, False).wait_send()

    for at, index in enumerate(handed):
        to_sibling(index, at, c).wait_send()
    swap_out.wait_send()


def on_device(
    queries, new_kv, prefix_kv, suffix_kv, suffix_len, parents, out_weight, residual,
    steer_dict, steer_ids, steer_strength, norm_gain, norm_bias,
):
    G = lax.axis_size("dp")
    Y = lax.axis_size("tensor")
    NX = X * C
    S = G * CAP
    B, width = queries.shape
    split, heads_a, heads_b = heads_of(width)
    wide = width - split
    heads2 = width // HEAD
    T = suffix_kv.shape[1]
    W = out_weight.shape[1]
    R = residual.shape[0]
    RC = R // C
    VM = pltpu.VMEM
    DMA = pltpu.SemaphoreType.DMA
    n_f = Y // X
    args = (
        queries, new_kv, prefix_kv, suffix_kv,
        (parents * PACK + suffix_len).reshape(G, B),
        out_weight.T, residual.T, steer_dict.T, steer_ids.T, steer_strength.T,
        norm_gain[None], norm_bias[None],
    )
    in_hbm = (1, 2, 3, 5, 7)
    big = max(NX, Z)
    scratch = (
        [VM((S, split), BF16)] * 4
        + [VM((S, wide), BF16)] * 4
        + [VM((S, split + HEAD), BF16)] * 4
        + [VM((S, wide + HEAD), BF16)] * 4
        + [
            VM((B, width), BF16), VM(new_kv.shape, BF16), VM(prefix_kv.shape, BF16), VM(suffix_kv.shape, BF16),
            VM((B * T, width), BF16), VM((B * T, width), BF16), VM(steer_dict.T.shape, BF16),
            VM((B, width), F32), VM((heads2, B, HEAD), F32), VM((heads2, B, HEAD), F32),
            VM((B, split), BF16), VM((B, wide), BF16),
            VM((X, Z // n_f, n_f, B, split), BF16), VM((X, Z // n_f, n_f, B, wide), BF16),
            VM((Y, C, W, width), BF16),
            VM((W, R), F32), VM((C, W, RC), F32), VM((C * W, RC), F32), VM((W, RC), F32),
            VM((8, RC), F32), VM((8, RC), F32), VM((NX, 8, RC), F32), VM((Z, 8, RC), F32),
        ]
        + [DMA((8, big))] * 2
        + [DMA((2, big))] * 2
        + [DMA((2, Y // 2))] * 2
        + [DMA((Y,))] * 2
        + [DMA((2, Z // 2))] * 2
        + [DMA((Z, 2, X // 2))] * 2
        + [DMA((2, X // 2))] * 2
        + [DMA((X, 2, Z // 2))] * 2
        + [DMA((4,))] * 2
        + [DMA((6,)), DMA, DMA]
    )
    out = pl.pallas_call(
        functools.partial(kernel, Y),
        out_shape=jax.ShapeDtypeStruct((W, R), BF16),
        in_specs=[pl.BlockSpec(memory_space=pl.ANY if i in in_hbm else VM) for i in range(len(args))],
        out_specs=pl.BlockSpec(memory_space=VM),
        scratch_shapes=scratch,
        compiler_params=pltpu.CompilerParams(
            collective_id=0, has_side_effects=True, vmem_limit_bytes=56 * 1024 * 1024
        ),
        name="beam_step",
    )(*args)
    return out.T


def solution(mesh):
    placed = (
        P("dp", "tensor"),
        P("dp", None, "tensor"),
        P(None, None, "tensor"),
        P("dp", None, None, "tensor"),
        P(),
        P(),
        P("tensor", "dp"),
        P("tensor", "dp"),
        P(None, "dp"),
        P("tensor", None),
        P("tensor", None),
        P("dp"),
        P("dp"),
    )
    return jax.shard_map(
        on_device, mesh=mesh, in_specs=placed, out_specs=P("tensor", "dp"), check_vma=False
    )
```

```python
import functools
import itertools

import jax
import jax.numpy as jnp
from jax import lax
from jax.experimental import pallas as pl
from jax.experimental.pallas import tpu as pltpu
from jax.sharding import PartitionSpec as P

MESH = pl.DeviceIdType.MESH
F32, BF16, I32 = jnp.float32, jnp.bfloat16, jnp.int32
D = 10240
HEAD = 128
CAP = 2
PACK = 16
X, Z, C = 4, 8, 2

NEG = -1e30
NT = (((1,), (1,)), ((), ()))
TN = (((0,), (0,)), ((), ()))


def iota(shape, dim):
    return lax.broadcasted_iota(I32, shape, dim)


def log2(n):
    return n.bit_length() - 1


def dot(a, b, dims=(((1,), (0,)), ((), ()))):
    return lax.dot_general(a, b, dims, preferred_element_type=F32)


def rows(start, size):
    return pl.ds(pl.multiple_of(start, size & -size), size)


def heads_of(width):
    heads = width // HEAD
    first = max(1, heads * 3 // 5)
    return first * HEAD, first, heads - first


class Exchange:
    def __init__(self, src, dst, n, me, peer_id, send, recv, chunk, chunk_of=lambda i: i):
        self.src, self.dst, self.n, self.me = src, dst, n, me
        self.peer_id, self.send, self.recv, self.chunk = peer_id, send, recv, chunk
        self.chunk_of = chunk_of

    def copy(self, k, to, out_at, in_at):
        return pltpu.make_async_remote_copy(
            src_ref=self.src.at[rows(out_at * self.chunk, self.chunk)],
            dst_ref=self.dst.at[rows(in_at * self.chunk, self.chunk)],
            send_sem=self.send.at[k],
            recv_sem=self.recv.at[k],
            device_id=self.peer_id(to),
            device_id_type=MESH,
        )

    def start(self):
        n, me = self.n, self.me

        def step(k, _):
            to = lax.rem(me + k, n)
            self.copy(k, to, self.chunk_of(to), me).start()
            return 0

        lax.fori_loop(1, n, step, 0)
        mine = self.src[rows(self.chunk_of(me) * self.chunk, self.chunk)]
        self.dst[rows(me * self.chunk, self.chunk)] = mine

    def wait(self):
        n, me = self.n, self.me

        def step(k, _):
            frm = lax.rem(me + n - k, n)
            self.copy(k, frm, frm, frm).wait_recv()
            return 0

        lax.fori_loop(1, n, step, 0)

    def drain(self):
        n, me = self.n, self.me

        def step(k, _):
            to = lax.rem(me + k, n)
            self.copy(k, to, self.chunk_of(to), me).wait_send()
            return 0

        lax.fori_loop(1, n, step, 0)


class Share(Exchange):
    def copy(self, k, to, out_at, in_at):
        return pltpu.make_async_remote_copy(
            src_ref=self.src,
            dst_ref=self.dst.at[in_at],
            send_sem=self.send.at[k],
            recv_sem=self.recv.at[k],
            device_id=self.peer_id(to),
            device_id_type=MESH,
        )

    def start(self):
        n, me = self.n, self.me

        def step(k, _):
            to = lax.rem(me + k, n)
            self.copy(k, to, to, me).start()
            return 0

        lax.fori_loop(1, n, step, 0)
        self.dst[me] = self.src[...]


class Ring:
    def __init__(self, view, n, me, peer_id, send, recv, split=False, last_way=0):
        self.view, self.n, self.me, self.peer_id = view, n, me, peer_id
        self.send, self.recv, self.split, self.last_way = send, recv, split, last_way
        self.steps = n // 2

    def moves(self, s):
        if s < 1 or s > self.steps:
            return []
        if 2 * s < self.n:
            return [(0, None), (1, None)]
        return [(0, 0), (1, 1)] if self.split else [(self.last_way, None)]

    def copy(self, s, way, part, index):
        ref = self.view(index, part)
        to = lax.rem(self.me + 1, self.n) if way == 0 else lax.rem(self.me + self.n - 1, self.n)
        return pltpu.make_async_remote_copy(
            src_ref=ref,
            dst_ref=ref,
            send_sem=self.send.at[way, s - 1],
            recv_sem=self.recv.at[way, s - 1],
            device_id=self.peer_id(to),
            device_id_type=MESH,
        )

    def at(self, offset):
        return lax.rem(self.me + offset + self.n, self.n)

    def outgoing(self, s):
        for way, part in self.moves(s):
            yield self.copy(s, way, part, self.at(1 - s if way == 0 else s - 1))

    def start(self, s):
        for c in self.outgoing(s):
            c.start()

    def wait(self, s):
        for way, part in self.moves(s):
            self.copy(s, way, part, self.at(-s if way == 0 else s)).wait_recv()

    def drain(self):
        for s in range(1, self.steps + 1):
            for c in self.outgoing(s):
                c.wait_send()


def three_terms(value):
    top = value.astype(BF16).astype(F32)
    rest = value - top
    middle = rest.astype(BF16).astype(F32)
    return top, middle, rest - middle


def kernel(
    Y,
    q_ref, new_hbm, pre_hbm, suf_hbm, par_ref,
    w_hbm, res_ref, dict_hbm, ids_ref, str_ref, gain_ref, bias_ref,
    out_ref,
    qs_a, q1_a, q2_a, q3_a, qs_b, q1_b, q2_b, q3_b,
    rs_a, r1_a, r2_a, r3_a, rs_b, r1_b, r2_b, r3_b,
    own_part, part, new_raw, pre_raw, suf_raw, sk_ref, sv_ref, dict_ref,
    att_a, att_b, ag_a, ag_b, wbuf, base, base_c, acc, sib, st1, st2, g1, g2,
    ex_send, ex_recv, sh_send, sh_recv, y_send, y_recv, ws_send, ws_recv,
    az_send, az_recv, ax_send, ax_recv, bx_send, bx_recv, bz_send, bz_recv,
    pm_send, pm_recv, in_sem, sb_send, sb_recv,
):
    NX = X * C
    G = NX * Z
    S = G * CAP
    B, width = q_ref.shape
    split, heads_a, heads_b = heads_of(width)
    wide = width - split
    n_a = X * Z // Y
    n_f = Z // n_a
    W = w_hbm.shape[0]
    R = res_ref.shape[1]
    RC = R // C
    scale = HEAD ** (-0.5)

    d = lax.axis_index("dp")
    y = lax.axis_index("tensor")
    c = lax.rem(d, C)
    p = lax.div(d, C)
    z = lax.rem(p, Z)
    x = lax.div(p, Z)
    xc = x * C + c

    def xc_id(i):
        return ((lax.div(i, C) * Z + z) * C + lax.rem(i, C), y)

    def z_id(i):
        return ((x * Z + i) * C + c, y)

    def x_id(i):
        return ((i * Z + z) * C + c, y)

    def y_id(i):
        return (d, i)

    sibling = (p * C + (1 - c), y)
    shift = (Z - n_a) // 2 // n_f * n_f

    def x_guest(i):
        return lax.rem(i - lax.div(y, n_f) + X, X)

    def z_guest(i):
        bit = lax.rem(i, n_f)
        low = lax.rem(bit - y + Y, n_f) * n_a
        return low + lax.div(lax.rem(i - bit - low + shift + Z, Z), n_f)

    z_half = lax.rem(lax.div(p, n_a), n_f)
    x_host = lax.rem(x + lax.div(y, n_f), X)
    z_host = lax.rem(
        z_half * n_a + n_f * lax.rem(z, n_a) - shift + lax.rem(y + z_half, n_f) + Z, Z
    )
    host = ((x_host * Z + z_host) * C + c, y)
    p_guest = x_guest(x) * Z + z_guest(z)
    d_guest = p_guest * C + c
    at_home = d_guest == d
    t_guest = lax.div(p_guest, n_a)

    def y_of(xi, bit):
        return n_f * lax.rem(xi - lax.div(y, n_f) + X, X) + lax.rem(bit - y + Y, n_f)

    y_from = y_of(x, lax.rem(z, n_f))
    in_plane = t_guest == y

    barrier = pltpu.get_barrier_semaphore()

    def hello(dev):
        pl.semaphore_signal(barrier, inc=1, device_id=dev, device_id_type=MESH)

    def greet(peer_id, n, me):
        def step(k, _):
            hello(peer_id(lax.rem(me + k, n)))
            return 0

        lax.fori_loop(1, n, step, 0)

    greet(xc_id, NX, xc)
    greet(z_id, Z, z)
    hello(y_id(lax.rem(y + 1, Y)))
    hello(y_id(lax.rem(y + Y - 1, Y)))


    @pl.when(jnp.logical_not(at_home))
    def _():
        hello((d_guest, y))

    @pl.when(jnp.logical_not(in_plane))
    def _():
        hello(y_id(y_from))

    loads = [
        pltpu.make_async_copy(a, b, in_sem.at[i])
        for i, (a, b) in enumerate((
            (w_hbm, wbuf.at[y, c]), (pre_hbm, pre_raw),
            (suf_hbm, suf_raw), (dict_hbm, dict_ref), (new_hbm, new_raw),
        ))
    ]
    for load in loads:
        load.start()

    r_bits = log2(CAP)
    slot = iota((S, 1), 0)
    rank_of = (slot & (CAP - 1)).astype(F32)
    group = slot >> r_bits
    xc_a, z_a = group >> log2(Z), group & (Z - 1)
    z_b, xc_b = group >> log2(NX), group & (NX - 1)

    def d_of(xc_, z_):
        return (((xc_ >> log2(C)) * Z + z_) * C + (xc_ & (C - 1))).astype(F32)

    d_a, d_b = d_of(xc_a, z_a), d_of(xc_b, z_b)
    before = (iota((B, B), 0) < iota((B, B), 1)).astype(BF16)

    def split_parents(par):
        par = par.astype(F32)
        both = jnp.floor(par * (1.0 / PACK))
        src = jnp.floor((both + 0.5) * (1.0 / B))
        return src, both - src * B, par - both * PACK

    def slots_of(block_src, dest):
        hit = block_src == dest
        rank = dot(hit.astype(BF16), before)
        return (hit & (rank == rank_of)).astype(BF16)

    my_src, _, my_len = split_parents(par_ref[pl.ds(d, 1), :])
    e_a, e_b = slots_of(my_src, d_a), slots_of(my_src, d_b)
    qs_a[...] = dot(e_a, q_ref[:, :split]).astype(BF16)
    qs_b[...] = dot(e_b, q_ref[:, split:]).astype(BF16)

    pl.semaphore_wait(
        barrier, NX - 1 + Z - 1 + 2 + jnp.where(at_home, 0, 1) + jnp.where(in_plane, 0, 1)
    )

    exchanges = []

    def exchange(src, dst, over_z, index, chunk, chunk_of=lambda i: i):
        n, me, peer = (Z, z, z_id) if over_z else (NX, xc, xc_id)
        e = Exchange(src, dst, n, me, peer, ex_send.at[index], ex_recv.at[index], chunk, chunk_of)
        exchanges.append(e)
        return e

    def xc_guest(i):
        return x_guest(lax.div(i, C)) * C + lax.rem(i, C)

    ca, cb = Z * CAP, NX * CAP
    e1a = exchange(qs_a, q1_a, False, 0, ca)
    e1b = exchange(qs_b, q1_b, True, 1, cb)
    e2a = exchange(q2_a, q3_a, True, 2, cb)
    e2b = exchange(q2_b, q3_b, False, 3, ca)
    e3a = exchange(rs_a, r1_a, True, 4, cb, z_guest)
    e3b = exchange(rs_b, r1_b, False, 5, ca, xc_guest)
    e4a = exchange(r2_a, r3_a, False, 6, ca, xc_guest)
    e4b = exchange(r2_b, r3_b, True, 7, cb, z_guest)

    e1a.start()
    e1b.start()

    def w_block(i, part):
        if part is None:
            return wbuf.at[i, c]
        return wbuf.at[i, c, pl.ds(part * (W // 2), W // 2)]

    loads[0].wait()
    wring = Ring(w_block, Y, y, y_id, y_send, y_recv, True)

    def to_sibling(index, at, core):
        ref = wbuf.at[index, core]
        return pltpu.make_async_remote_copy(
            src_ref=ref, dst_ref=ref, send_sem=ws_send.at[at], recv_sem=ws_recv.at[at],
            device_id=sibling, device_id_type=MESH,
        )

    handed = []

    def hand(offset):
        index = lax.rem(y + offset + Y, Y)
        at = len(handed)
        to_sibling(index, at, c).start()
        handed.append(index)

    wring.start(1)
    hand(0)

    def w_step(s):
        wring.wait(s)
        if s < wring.steps:
            wring.start(s + 1)
        hand(-s)
        if 2 * s < Y:
            hand(s)

    loads[1].wait()
    loads[4].wait()
    all_heads = heads_a + heads_b
    lane_b = iota((B, HEAD), 1)
    logs = jnp.zeros((B, HEAD), F32)
    for h in range(all_heads):
        cols = slice(h * HEAD, (h + 1) * HEAD)
        qh = q_ref[:, cols]
        pre = pre_raw[:, :, cols].astype(F32)
        new = new_raw[:, :, cols].astype(F32)
        s_pre = dot(qh, pre[:, 0].astype(BF16), NT) * scale
        m_pre = jnp.max(s_pre, axis=1, keepdims=True)
        e_pre = jnp.exp(s_pre - m_pre)
        l_pre = jnp.sum(e_pre, axis=1, keepdims=True)
        o_pre = dot(e_pre.astype(BF16), pre[:, 1].astype(BF16))
        s_self = scale * jnp.sum(qh.astype(F32) * new[:, 0], axis=1, keepdims=True)
        m1 = jnp.maximum(m_pre, s_self)
        up, us = jnp.exp(m_pre - m1), jnp.exp(s_self - m1)
        den = up * l_pre + us
        own_part[:, cols] = ((up * o_pre + us * new[:, 1]) / den).astype(BF16)
        for k, term in enumerate(three_terms(m1 + jnp.log(den))):
            logs = jnp.where(lane_b == k * all_heads + h, term, logs)
    own_part[:, width:] = logs.astype(BF16)

    keys = sk_ref.shape[0]
    loads[2].wait()
    for h in range(heads_a + heads_b):
        cols = slice(h * HEAD, (h + 1) * HEAD)
        pair = suf_raw[:, :, :, cols].astype(F32)
        sk_ref[:, cols] = pair[:, :, 0].reshape(keys, HEAD).astype(BF16)
        sv_ref[:, cols] = pair[:, :, 1].reshape(keys, HEAD).astype(BF16)

    out_i, in_j = iota((S, S), 0), iota((S, S), 1)

    def swap(n_out, n_in):
        g = out_i >> r_bits
        u, v = g >> log2(n_in), g & (n_in - 1)
        return (in_j == ((v * n_out + u) * CAP + (out_i & (CAP - 1)))).astype(BF16)

    to_b, to_a = swap(Z, NX), swap(NX, Z)

    e1a.wait()
    q2_a[...] = dot(to_b, q1_a[...]).astype(BF16)
    e2a.start()
    e1b.wait()
    q2_b[...] = dot(to_a, q1_b[...]).astype(BF16)
    e2b.start()

    src, off, _ = split_parents(par_ref[...])
    group_of = iota((S, G), 1).astype(F32)
    T = keys // B
    beam_of = iota((B, keys), 1) >> log2(T)
    spread = (beam_of == iota((B, keys), 0)).astype(BF16)
    live = dot(my_len.astype(BF16), spread)
    live_cols = (iota((1, keys), 1) & (T - 1)).astype(F32) < live
    col_beam = (iota((1, keys), 1) >> log2(T)).astype(F32)
    here = d.astype(F32)

    def mask_of(dest):
        pick = (group_of == dest).astype(BF16)
        hit = dot(pick, src.astype(BF16)) == here
        rank = dot(hit.astype(BF16), before)
        chosen = (hit & (rank == rank_of)).astype(F32)
        offset = jnp.sum(chosen * dot(pick, off.astype(BF16)), axis=1, keepdims=True)
        there = jnp.sum(chosen, axis=1, keepdims=True) > 0.0
        offset = jnp.where(there, offset, -1.0)
        return (offset == col_beam) & live_cols

    feats = dict_ref.shape[1]
    step_f = min(feats, 128)
    base[...] = res_ref[...].astype(F32)
    loads[3].wait()

    def steer(i, _):
        at = i * step_f
        feature = iota((step_f, R), 0) + at
        s = jnp.zeros((step_f, R), F32)
        for k in range(ids_ref.shape[0]):
            s = s + jnp.where(feature == ids_ref[k : k + 1, :], str_ref[k : k + 1, :], 0.0)
        top, middle, _ = three_terms(s)
        part = dict_ref[:, rows(at, step_f)]
        base[...] += dot(part, top.astype(BF16)) + dot(part, middle.astype(BF16))
        return 0

    lax.fori_loop(0, feats // step_f, steer, 0)

    ri, ci = iota((RC, R), 0), iota((RC, R), 1)
    turn = n_a - lax.rem(y, n_f) * (n_a // n_f) + shift // n_f
    block_no = sum((ri >= B * k).astype(I32) for k in range(1, n_a))
    place_no = (block_no + turn) & (n_a - 1)

    def spot(core):
        return (ci == (place_no * C + core) * B + ri - block_no * B).astype(F32)

    for k in range(C):
        base_c[k] = lax.dot_general(
            base[...], spot(k), NT, preferred_element_type=F32, precision=lax.Precision.HIGHEST
        )

    def attend(q3, mask, rs, first, heads):
        lane = iota((S, HEAD), 1)
        extra = jnp.zeros((S, HEAD), F32)
        for i in range(heads):
            cols = slice((first + i) * HEAD, (first + i + 1) * HEAD)
            mine = slice(i * HEAD, (i + 1) * HEAD)
            s = dot(q3[:, mine], sk_ref[:, cols], NT) * scale
            s = jnp.where(mask, s, NEG)
            m = jnp.max(s, axis=1, keepdims=True)
            e = jnp.where(mask, jnp.exp(s - m), 0.0)
            l = jnp.maximum(jnp.sum(e, axis=1, keepdims=True), 1e-30)
            o = dot(e.astype(BF16), sv_ref[:, cols]) / l
            rs[:, mine] = o.astype(BF16)
            for k, term in enumerate(three_terms(m + jnp.log(l))):
                extra = jnp.where(lane == k * heads + i, term, extra)
        rs[:, heads * HEAD :] = extra.astype(BF16)

    mask_b, mask_a = mask_of(d_b), mask_of(d_a)

    w_step(1)
    e2a.wait()
    lodge = pltpu.make_async_remote_copy(
        src_ref=own_part, dst_ref=part, send_sem=pm_send.at[2], recv_sem=pm_recv.at[2],
        device_id=host, device_id_type=MESH,
    )

    @pl.when(at_home)
    def _():
        part[...] = own_part[...]

    @pl.when(jnp.logical_not(at_home))
    def _():
        lodge.start()

    attend(q3_a, mask_b, rs_a, 0, heads_a)
    e3a.start()
    e2b.wait()
    attend(q3_b, mask_a, rs_b, heads_a, heads_b)
    e3b.start()

    if wring.steps > 1:
        w_step(2)
    e3a.wait()
    r2_a[...] = dot(to_a, r1_a[...]).astype(BF16)
    e4a.start()
    e3b.wait()
    r2_b[...] = dot(to_b, r1_b[...]).astype(BF16)
    e4b.start()
    def merge(e, r3, att, first, heads):
        got = dot(e, r3[...], TN)
        for i in range(heads):
            h = first + i
            mine = slice(i * HEAD, (i + 1) * HEAD)
            extra = heads * HEAD + i
            lse = sum(got[:, extra + k * heads : extra + k * heads + 1] for k in range(3))
            lse1 = sum(
                part[:, at : at + 1].astype(F32)
                for at in (width + k * (heads_a + heads_b) + h for k in range(3))
            )
            m = jnp.maximum(lse1, lse)
            a, b = jnp.exp(lse1 - m), jnp.exp(lse - m)
            total = a * part[:, h * HEAD : (h + 1) * HEAD].astype(F32) + b * got[:, mine]
            att[:, mine] = (total / (a + b)).astype(BF16)

    def block_a(xi, zi):
        return ag_a.at[xi, lax.div(zi, n_f), lax.rem(zi, n_f)]

    def block_b(xi, zi):
        return ag_b.at[xi, lax.div(zi, n_f), lax.rem(zi, n_f)]

    def place(att, block, at):
        return pltpu.make_async_remote_copy(
            src_ref=att, dst_ref=block(x, z),
            send_sem=pm_send.at[at], recv_sem=pm_recv.at[at],
            device_id=y_id(t_guest), device_id_type=MESH,
        )

    def move(att, block, at):
        @pl.when(in_plane)
        def _():
            block(x, z)[...] = att[...]

        @pl.when(jnp.logical_not(in_plane))
        def _():
            place(att, block, at).start()

    def settle(att, block, at):
        @pl.when(jnp.logical_not(in_plane))
        def _():
            place(att, block, at).wait_recv()

    guest_src, _, _ = split_parents(par_ref[pl.ds(d_guest, 1), :])
    f_a, f_b = slots_of(guest_src, d_a), slots_of(guest_src, d_b)
    @pl.when(jnp.logical_not(at_home))
    def _():
        lodge.wait_recv()

    e4a.wait()
    merge(f_a, r3_a, att_a, 0, heads_a)
    move(att_a, block_a, 0)
    e4b.wait()
    merge(f_b, r3_b, att_b, heads_a, heads_b)
    move(att_b, block_b, 1)

    class Spread:
        def __init__(self, along, across):
            self.along, self.across = along, across

        def jobs(self, r):
            def source():
                if r:
                    self.along.wait(r)
                self.along.start(r + 1)
                fresh = [0] if r == 0 else [-r, r][: 1 if 2 * r == self.along.n else 2]
                if r <= self.along.steps:
                    for o in fresh:
                        self.across[o].start(1)

            def pass_on(ring, step):
                ring.wait(step)
                ring.start(step + 1)

            yield source
            for o, ring in self.across.items():
                if 0 < r - abs(o) <= ring.steps:
                    yield functools.partial(pass_on, ring, r - abs(o))

        def drain(self):
            self.along.drain()
            for ring in self.across.values():
                ring.drain()

    def offsets(n):
        return [0] + [o for k in range(1, n // 2 + 1) for o in ([-k, k] if 2 * k < n else [-k])]

    spread_a = Spread(
        Ring(lambda i, part: block_a(x, i), Z, z, z_id, az_send, az_recv),
        {
            o: Ring(
                lambda i, part, o=o: block_a(i, lax.rem(z + o + Z, Z)),
                X, x, x_id, ax_send.at[k], ax_recv.at[k], last_way=k % 2,
            )
            for k, o in enumerate(offsets(Z))
        },
    )
    spread_b = Spread(
        Ring(lambda i, part: block_b(i, z), X, x, x_id, bx_send, bx_recv),
        {
            o: Ring(
                lambda i, part, o=o: block_b(lax.rem(x + o + X, X), i),
                Z, z, z_id, bz_send.at[k], bz_recv.at[k], last_way=1 - k % 2,
            )
            for k, o in enumerate(offsets(X))
        },
    )
    rounds = (X + Z) // 2

    def multiply(xi, first):
        for bit in range(n_f):
            ys = y_of(xi, bit)
            for ag, at, size in ((ag_a, 0, split), (ag_b, split, wide)):
                weights = wbuf[ys, :, :, at : at + size].reshape(C * W, size)
                part = dot(weights, ag[xi, :, bit].reshape(n_a * B, size), NT)
                if first and bit == 0 and at == 0:
                    acc[...] = part
                else:
                    acc[...] += part

    def weights_here():
        for at, index in enumerate(handed):
            to_sibling(index, at, 1 - c).wait_recv()

    for r in range(rounds + 1):
        if r == 0:
            settle(att_a, block_a, 0)
        for job_a, job_b in itertools.zip_longest(spread_a.jobs(r), spread_b.jobs(r)):
            if job_a:
                job_a()
            if r == 0 and job_b:
                settle(att_b, block_b, 1)
            if job_b:
                job_b()
        if r == 0 and wring.steps > 2:
            w_step(3)
        if r == Z // 4 and wring.steps > 3:
            w_step(4)
        if r == Z // 2:
            weights_here()
        if r >= Z // 2:
            k = r - Z // 2
            multiply(lax.rem(x + k, X), k == 0)
            if 0 < 2 * k < X:
                multiply(lax.rem(x + X - k, X), False)

    swap_out = pltpu.make_async_remote_copy(
        src_ref=acc.at[rows((1 - c) * W, W)], dst_ref=sib,
        send_sem=sb_send, recv_sem=sb_recv, device_id=sibling, device_id_type=MESH,
    )
    swap_out.start()
    acc[rows(c * W, W), :] += base_c[c]

    def join(got, n_each, core):
        n = got.shape[0]
        means, squares = got[:, 2 * core : 2 * core + 1, :], got[:, 2 * core + 1 : 2 * core + 2, :]
        mean = jnp.sum(means, axis=0) * (1.0 / n)
        away = means - mean[None]
        square = jnp.sum(squares, axis=0) + n_each * jnp.sum(away * away, axis=0)
        return mean, square

    row_no = iota((8, RC), 0)

    def pack(stats, core):
        mean, square = stats
        return jnp.where(row_no == core * 2, mean, jnp.where(row_no == core * 2 + 1, square, 0.0))

    def stats_of(value):
        mean = jnp.sum(value, axis=0, keepdims=True) * (1.0 / W)
        away = value - mean
        return mean, jnp.sum(away * away, axis=0, keepdims=True)

    mine = pack(stats_of(acc[rows(c * W, W), :]), c)
    swap_out.wait_recv()
    sib[...] += base_c[1 - c]
    st1[...] = mine + pack(stats_of(sib[...]), 1 - c)
    s1 = Share(st1, g1, NX, xc, xc_id, sh_send.at[0], sh_recv.at[0], 1)
    s1.start()
    eye = iota((W, W), 0) == iota((W, W), 1)
    gain = jnp.sum(jnp.where(eye, gain_ref[...], 0.0), axis=1, keepdims=True)
    bias = jnp.sum(jnp.where(eye, bias_ref[...], 0.0), axis=1, keepdims=True)
    s1.wait()
    st2[...] = sum(pack(join(g1[...], float(W), k), k) for k in range(C))
    s2 = Share(st2, g2, Z, z, z_id, sh_send.at[1], sh_recv.at[1], 1)
    s2.start()
    s2.wait()
    def normed(value, core):
        mean, square = joined[core]
        var = square * (1.0 / (W * NX * Z))
        return ((value - mean) * lax.rsqrt(var + 1e-5) * gain + bias).astype(BF16)

    joined = [join(g2[...], float(W * NX), k) for k in range(C)]
    own = acc[rows(c * W, W), :]
    parts = [normed(jnp.where(c == k, own, sib[...]), k) for k in range(C)]
    out_ref[...] = sum(dot(part, spot(k).astype(BF16)) for k, part in enumerate(parts)).astype(BF16)

    for e in exchanges:
        e.drain()
    s1.drain()
    s2.drain()
    for ring in (wring, spread_a, spread_b):
        ring.drain()

    @pl.when(jnp.logical_not(in_plane))
    def _():
        place(att_a, block_a, 0).wait_send()
        place(att_b, block_b, 1).wait_send()

    @pl.when(jnp.logical_not(at_home))
    def _():
        lodge.wait_send()

    for at, index in enumerate(handed):
        to_sibling(index, at, c).wait_send()
    swap_out.wait_send()


def on_device(
    queries, new_kv, prefix_kv, suffix_kv, suffix_len, parents, out_weight, residual,
    steer_dict, steer_ids, steer_strength, norm_gain, norm_bias,
):
    G = lax.axis_size("dp")
    Y = lax.axis_size("tensor")
    NX = X * C
    S = G * CAP
    B, width = queries.shape
    split, heads_a, heads_b = heads_of(width)
    wide = width - split
    T = suffix_kv.shape[1]
    W = out_weight.shape[1]
    R = residual.shape[0]
    RC = R // C
    VM = pltpu.VMEM
    DMA = pltpu.SemaphoreType.DMA
    n_f = Y // X
    args = (
        queries, new_kv, prefix_kv, suffix_kv,
        (parents * PACK + suffix_len).reshape(G, B),
        out_weight.T, residual.T, steer_dict.T, steer_ids.T, steer_strength.T,
        norm_gain[None], norm_bias[None],
    )
    in_hbm = (1, 2, 3, 5, 7)
    big = max(NX, Z)
    scratch = (
        [VM((S, split), BF16)] * 4
        + [VM((S, wide), BF16)] * 4
        + [VM((S, split + HEAD), BF16)] * 4
        + [VM((S, wide + HEAD), BF16)] * 4
        + [
            VM((B, width + HEAD), BF16), VM((B, width + HEAD), BF16), VM(new_kv.shape, BF16), VM(prefix_kv.shape, BF16), VM(suffix_kv.shape, BF16),
            VM((B * T, width), BF16), VM((B * T, width), BF16), VM(steer_dict.T.shape, BF16),
            VM((B, split), BF16), VM((B, wide), BF16),
            VM((X, Z // n_f, n_f, B, split), BF16), VM((X, Z // n_f, n_f, B, wide), BF16),
            VM((Y, C, W, width), BF16),
            VM((W, R), F32), VM((C, W, RC), F32), VM((C * W, RC), F32), VM((W, RC), F32),
            VM((8, RC), F32), VM((8, RC), F32), VM((NX, 8, RC), F32), VM((Z, 8, RC), F32),
        ]
        + [DMA((8, big))] * 2
        + [DMA((2, big))] * 2
        + [DMA((2, Y // 2))] * 2
        + [DMA((Y,))] * 2
        + [DMA((2, Z // 2))] * 2
        + [DMA((Z, 2, X // 2))] * 2
        + [DMA((2, X // 2))] * 2
        + [DMA((X, 2, Z // 2))] * 2
        + [DMA((4,))] * 2
        + [DMA((6,)), DMA, DMA]
    )
    out = pl.pallas_call(
        functools.partial(kernel, Y),
        out_shape=jax.ShapeDtypeStruct((W, R), BF16),
        in_specs=[pl.BlockSpec(memory_space=pl.ANY if i in in_hbm else VM) for i in range(len(args))],
        out_specs=pl.BlockSpec(memory_space=VM),
        scratch_shapes=scratch,
        compiler_params=pltpu.CompilerParams(
            collective_id=0, has_side_effects=True, vmem_limit_bytes=56 * 1024 * 1024
        ),
        name="beam_step",
    )(*args)
    return out.T


def solution(mesh):
    placed = (
        P("dp", "tensor"),
        P("dp", None, "tensor"),
        P(None, None, "tensor"),
        P("dp", None, None, "tensor"),
        P(),
        P(),
        P("tensor", "dp"),
        P("tensor", "dp"),
        P(None, "dp"),
        P("tensor", None),
        P("tensor", None),
        P("dp"),
        P("dp"),
    )
    return jax.shard_map(
        on_device, mesh=mesh, in_specs=placed, out_specs=P("tensor", "dp"), check_vma=False
    )
```

```python
import functools
import itertools

import jax
import jax.numpy as jnp
from jax import lax
from jax.experimental import pallas as pl
from jax.experimental.pallas import tpu as pltpu
from jax.sharding import PartitionSpec as P

MESH = pl.DeviceIdType.MESH
F32, BF16, I32 = jnp.float32, jnp.bfloat16, jnp.int32
D = 10240
HEAD = 128
CAP = 2
PACK = 16
X, Z, C = 4, 8, 2

NEG = -1e30
NT = (((1,), (1,)), ((), ()))
TN = (((0,), (0,)), ((), ()))


def iota(shape, dim):
    return lax.broadcasted_iota(I32, shape, dim)


def log2(n):
    return n.bit_length() - 1


def dot(a, b, dims=(((1,), (0,)), ((), ()))):
    return lax.dot_general(a, b, dims, preferred_element_type=F32)


def rows(start, size):
    return pl.ds(pl.multiple_of(start, size & -size), size)


def heads_of(width):
    heads = width // HEAD
    first = max(1, heads * 3 // 5)
    return first * HEAD, first, heads - first


def far_first(i, n):
    half = lax.div(i + 1, 2)
    return n // 2 + half - 2 * half * lax.rem(i + 1, 2)


class Exchange:
    def __init__(self, src, dst, n, me, peer_id, send, recv, chunk, chunk_of=lambda i: i):
        self.src, self.dst, self.n, self.me = src, dst, n, me
        self.peer_id, self.send, self.recv, self.chunk = peer_id, send, recv, chunk
        self.chunk_of = chunk_of

    def copy(self, k, to, out_at, in_at):
        return pltpu.make_async_remote_copy(
            src_ref=self.src.at[rows(out_at * self.chunk, self.chunk)],
            dst_ref=self.dst.at[rows(in_at * self.chunk, self.chunk)],
            send_sem=self.send.at[k],
            recv_sem=self.recv.at[k],
            device_id=self.peer_id(to),
            device_id_type=MESH,
        )

    def start(self):
        n, me = self.n, self.me

        def step(i, _):
            k = far_first(i, n)
            to = lax.rem(me + k, n)
            self.copy(k, to, self.chunk_of(to), me).start()
            return 0

        lax.fori_loop(0, n - 1, step, 0)
        mine = self.src[rows(self.chunk_of(me) * self.chunk, self.chunk)]
        self.dst[rows(me * self.chunk, self.chunk)] = mine

    def wait(self):
        n, me = self.n, self.me

        def step(k, _):
            frm = lax.rem(me + n - k, n)
            self.copy(k, frm, frm, frm).wait_recv()
            return 0

        lax.fori_loop(1, n, step, 0)

    def drain(self):
        n, me = self.n, self.me

        def step(k, _):
            to = lax.rem(me + k, n)
            self.copy(k, to, self.chunk_of(to), me).wait_send()
            return 0

        lax.fori_loop(1, n, step, 0)


class Share(Exchange):
    def copy(self, k, to, out_at, in_at):
        return pltpu.make_async_remote_copy(
            src_ref=self.src,
            dst_ref=self.dst.at[in_at],
            send_sem=self.send.at[k],
            recv_sem=self.recv.at[k],
            device_id=self.peer_id(to),
            device_id_type=MESH,
        )

    def start(self):
        n, me = self.n, self.me

        def step(i, _):
            k = far_first(i, n)
            to = lax.rem(me + k, n)
            self.copy(k, to, to, me).start()
            return 0

        lax.fori_loop(0, n - 1, step, 0)
        self.dst[me] = self.src[...]


class Ring:
    def __init__(self, view, n, me, peer_id, send, recv, split=False, last_way=0):
        self.view, self.n, self.me, self.peer_id = view, n, me, peer_id
        self.send, self.recv, self.split, self.last_way = send, recv, split, last_way
        self.steps = n // 2

    def moves(self, s):
        if s < 1 or s > self.steps:
            return []
        if 2 * s < self.n:
            return [(0, None), (1, None)]
        return [(0, 0), (1, 1)] if self.split else [(self.last_way, None)]

    def copy(self, s, way, part, index):
        ref = self.view(index, part)
        to = lax.rem(self.me + 1, self.n) if way == 0 else lax.rem(self.me + self.n - 1, self.n)
        return pltpu.make_async_remote_copy(
            src_ref=ref,
            dst_ref=ref,
            send_sem=self.send.at[way, s - 1],
            recv_sem=self.recv.at[way, s - 1],
            device_id=self.peer_id(to),
            device_id_type=MESH,
        )

    def at(self, offset):
        return lax.rem(self.me + offset + self.n, self.n)

    def outgoing(self, s):
        for way, part in self.moves(s):
            yield self.copy(s, way, part, self.at(1 - s if way == 0 else s - 1))

    def start(self, s):
        for c in self.outgoing(s):
            c.start()

    def wait(self, s):
        for way, part in self.moves(s):
            self.copy(s, way, part, self.at(-s if way == 0 else s)).wait_recv()

    def drain(self):
        for s in range(1, self.steps + 1):
            for c in self.outgoing(s):
                c.wait_send()


def three_terms(value):
    top = value.astype(BF16).astype(F32)
    rest = value - top
    middle = rest.astype(BF16).astype(F32)
    return top, middle, rest - middle


def kernel(
    Y,
    q_ref, new_hbm, pre_hbm, suf_hbm, par_ref,
    w_hbm, res_ref, dict_hbm, ids_ref, str_ref, gain_ref, bias_ref,
    out_ref,
    qs_a, q1_a, q2_a, q3_a, qs_b, q1_b, q2_b, q3_b,
    rs_a, r1_a, r2_a, r3_a, rs_b, r1_b, r2_b, r3_b,
    own_part, part, new_raw, pre_raw, suf_raw, sk_ref, sv_ref, dict_ref,
    att_a, att_b, ag_a, ag_b, wbuf, base, base_c, acc, sib, st1, st2, g1, g2,
    ex_send, ex_recv, sh_send, sh_recv, y_send, y_recv, ws_send, ws_recv,
    az_send, az_recv, ax_send, ax_recv, bx_send, bx_recv, bz_send, bz_recv,
    pm_send, pm_recv, in_sem, sb_send, sb_recv,
):
    NX = X * C
    G = NX * Z
    S = G * CAP
    B, width = q_ref.shape
    split, heads_a, heads_b = heads_of(width)
    wide = width - split
    n_a = X * Z // Y
    n_f = Z // n_a
    W = w_hbm.shape[0]
    R = res_ref.shape[1]
    RC = R // C
    scale = HEAD ** (-0.5)

    d = lax.axis_index("dp")
    y = lax.axis_index("tensor")
    c = lax.rem(d, C)
    p = lax.div(d, C)
    z = lax.rem(p, Z)
    x = lax.div(p, Z)
    xc = x * C + c

    def xc_id(i):
        return ((lax.div(i, C) * Z + z) * C + lax.rem(i, C), y)

    def z_id(i):
        return ((x * Z + i) * C + c, y)

    def x_id(i):
        return ((i * Z + z) * C + c, y)

    def y_id(i):
        return (d, i)

    sibling = (p * C + (1 - c), y)
    shift = (Z - n_a) // 2 // n_f * n_f

    def x_guest(i):
        return lax.rem(i - lax.div(y, n_f) + X, X)

    def z_guest(i):
        bit = lax.rem(i, n_f)
        low = lax.rem(bit - y + Y, n_f) * n_a
        return low + lax.div(lax.rem(i - bit - low + shift + Z, Z), n_f)

    z_half = lax.rem(lax.div(p, n_a), n_f)
    x_host = lax.rem(x + lax.div(y, n_f), X)
    z_host = lax.rem(
        z_half * n_a + n_f * lax.rem(z, n_a) - shift + lax.rem(y + z_half, n_f) + Z, Z
    )
    host = ((x_host * Z + z_host) * C + c, y)
    p_guest = x_guest(x) * Z + z_guest(z)
    d_guest = p_guest * C + c
    at_home = d_guest == d
    t_guest = lax.div(p_guest, n_a)

    def y_of(xi, bit):
        return n_f * lax.rem(xi - lax.div(y, n_f) + X, X) + lax.rem(bit - y + Y, n_f)

    y_from = y_of(x, lax.rem(z, n_f))
    in_plane = t_guest == y

    barrier = pltpu.get_barrier_semaphore()

    def hello(dev):
        pl.semaphore_signal(barrier, inc=1, device_id=dev, device_id_type=MESH)

    def greet(peer_id, n, me):
        def step(k, _):
            hello(peer_id(lax.rem(me + k, n)))
            return 0

        lax.fori_loop(1, n, step, 0)

    greet(xc_id, NX, xc)
    greet(z_id, Z, z)
    hello(y_id(lax.rem(y + 1, Y)))
    hello(y_id(lax.rem(y + Y - 1, Y)))


    @pl.when(jnp.logical_not(at_home))
    def _():
        hello((d_guest, y))

    @pl.when(jnp.logical_not(in_plane))
    def _():
        hello(y_id(y_from))

    loads = [
        pltpu.make_async_copy(a, b, in_sem.at[i])
        for i, (a, b) in enumerate((
            (w_hbm, wbuf.at[y, c]), (pre_hbm, pre_raw),
            (suf_hbm, suf_raw), (dict_hbm, dict_ref), (new_hbm, new_raw),
        ))
    ]
    for load in loads:
        load.start()

    r_bits = log2(CAP)
    slot = iota((S, 1), 0)
    rank_of = (slot & (CAP - 1)).astype(F32)
    group = slot >> r_bits
    xc_a, z_a = group >> log2(Z), group & (Z - 1)
    z_b, xc_b = group >> log2(NX), group & (NX - 1)

    def d_of(xc_, z_):
        return (((xc_ >> log2(C)) * Z + z_) * C + (xc_ & (C - 1))).astype(F32)

    d_a, d_b = d_of(xc_a, z_a), d_of(xc_b, z_b)
    before = (iota((B, B), 0) < iota((B, B), 1)).astype(BF16)

    def split_parents(par):
        par = par.astype(F32)
        both = jnp.floor(par * (1.0 / PACK))
        src = jnp.floor((both + 0.5) * (1.0 / B))
        return src, both - src * B, par - both * PACK

    def slots_of(block_src, dest):
        hit = block_src == dest
        rank = dot(hit.astype(BF16), before)
        return (hit & (rank == rank_of)).astype(BF16)

    my_src, _, my_len = split_parents(par_ref[pl.ds(d, 1), :])
    e_a, e_b = slots_of(my_src, d_a), slots_of(my_src, d_b)
    qs_a[...] = dot(e_a, q_ref[:, :split]).astype(BF16)
    qs_b[...] = dot(e_b, q_ref[:, split:]).astype(BF16)

    pl.semaphore_wait(
        barrier, NX - 1 + Z - 1 + 2 + jnp.where(at_home, 0, 1) + jnp.where(in_plane, 0, 1)
    )

    exchanges = []

    def exchange(src, dst, over_z, index, chunk, chunk_of=lambda i: i):
        n, me, peer = (Z, z, z_id) if over_z else (NX, xc, xc_id)
        e = Exchange(src, dst, n, me, peer, ex_send.at[index], ex_recv.at[index], chunk, chunk_of)
        exchanges.append(e)
        return e

    def xc_guest(i):
        return x_guest(lax.div(i, C)) * C + lax.rem(i, C)

    ca, cb = Z * CAP, NX * CAP
    e1a = exchange(qs_a, q1_a, False, 0, ca)
    e1b = exchange(qs_b, q1_b, True, 1, cb)
    e2a = exchange(q2_a, q3_a, True, 2, cb)
    e2b = exchange(q2_b, q3_b, False, 3, ca)
    e3a = exchange(rs_a, r1_a, True, 4, cb, z_guest)
    e3b = exchange(rs_b, r1_b, False, 5, ca, xc_guest)
    e4a = exchange(r2_a, r3_a, False, 6, ca, xc_guest)
    e4b = exchange(r2_b, r3_b, True, 7, cb, z_guest)

    e1a.start()
    e1b.start()

    def w_block(i, part):
        if part is None:
            return wbuf.at[i, c]
        return wbuf.at[i, c, pl.ds(part * (W // 2), W // 2)]

    loads[0].wait()
    wring = Ring(w_block, Y, y, y_id, y_send, y_recv, True)

    def to_sibling(index, at, core):
        ref = wbuf.at[index, core]
        return pltpu.make_async_remote_copy(
            src_ref=ref, dst_ref=ref, send_sem=ws_send.at[at], recv_sem=ws_recv.at[at],
            device_id=sibling, device_id_type=MESH,
        )

    handed = []

    def hand(offset):
        index = lax.rem(y + offset + Y, Y)
        at = len(handed)
        to_sibling(index, at, c).start()
        handed.append(index)

    wring.start(1)
    hand(0)

    def w_step(s):
        wring.wait(s)
        if s < wring.steps:
            wring.start(s + 1)
        hand(-s)
        if 2 * s < Y:
            hand(s)

    loads[1].wait()
    loads[4].wait()
    all_heads = heads_a + heads_b
    lane_b = iota((B, HEAD), 1)
    logs = jnp.zeros((B, HEAD), F32)
    for h in range(all_heads):
        cols = slice(h * HEAD, (h + 1) * HEAD)
        qh = q_ref[:, cols]
        pre = pre_raw[:, :, cols].astype(F32)
        new = new_raw[:, :, cols].astype(F32)
        s_pre = dot(qh, pre[:, 0].astype(BF16), NT) * scale
        m_pre = jnp.max(s_pre, axis=1, keepdims=True)
        e_pre = jnp.exp(s_pre - m_pre)
        l_pre = jnp.sum(e_pre, axis=1, keepdims=True)
        o_pre = dot(e_pre.astype(BF16), pre[:, 1].astype(BF16))
        s_self = scale * jnp.sum(qh.astype(F32) * new[:, 0], axis=1, keepdims=True)
        m1 = jnp.maximum(m_pre, s_self)
        up, us = jnp.exp(m_pre - m1), jnp.exp(s_self - m1)
        den = up * l_pre + us
        own_part[:, cols] = ((up * o_pre + us * new[:, 1]) / den).astype(BF16)
        for k, term in enumerate(three_terms(m1 + jnp.log(den))):
            logs = jnp.where(lane_b == k * all_heads + h, term, logs)
    own_part[:, width:] = logs.astype(BF16)

    keys = sk_ref.shape[0]
    loads[2].wait()
    for h in range(heads_a + heads_b):
        cols = slice(h * HEAD, (h + 1) * HEAD)
        pair = suf_raw[:, :, :, cols].astype(F32)
        sk_ref[:, cols] = pair[:, :, 0].reshape(keys, HEAD).astype(BF16)
        sv_ref[:, cols] = pair[:, :, 1].reshape(keys, HEAD).astype(BF16)

    out_i, in_j = iota((S, S), 0), iota((S, S), 1)

    def swap(n_out, n_in):
        g = out_i >> r_bits
        u, v = g >> log2(n_in), g & (n_in - 1)
        return (in_j == ((v * n_out + u) * CAP + (out_i & (CAP - 1)))).astype(BF16)

    to_b, to_a = swap(Z, NX), swap(NX, Z)

    e1a.wait()
    q2_a[...] = dot(to_b, q1_a[...]).astype(BF16)
    e2a.start()
    e1b.wait()
    q2_b[...] = dot(to_a, q1_b[...]).astype(BF16)
    e2b.start()

    src, off, _ = split_parents(par_ref[...])
    group_of = iota((S, G), 1).astype(F32)
    T = keys // B
    beam_of = iota((B, keys), 1) >> log2(T)
    spread = (beam_of == iota((B, keys), 0)).astype(BF16)
    live = dot(my_len.astype(BF16), spread)
    live_cols = (iota((1, keys), 1) & (T - 1)).astype(F32) < live
    col_beam = (iota((1, keys), 1) >> log2(T)).astype(F32)
    here = d.astype(F32)

    def mask_of(dest):
        pick = (group_of == dest).astype(BF16)
        hit = dot(pick, src.astype(BF16)) == here
        rank = dot(hit.astype(BF16), before)
        chosen = (hit & (rank == rank_of)).astype(F32)
        offset = jnp.sum(chosen * dot(pick, off.astype(BF16)), axis=1, keepdims=True)
        there = jnp.sum(chosen, axis=1, keepdims=True) > 0.0
        offset = jnp.where(there, offset, -1.0)
        return (offset == col_beam) & live_cols

    feats = dict_ref.shape[1]
    step_f = min(feats, 128)
    base[...] = res_ref[...].astype(F32)
    loads[3].wait()

    def steer(i, _):
        at = i * step_f
        feature = iota((step_f, R), 0) + at
        s = jnp.zeros((step_f, R), F32)
        for k in range(ids_ref.shape[0]):
            s = s + jnp.where(feature == ids_ref[k : k + 1, :], str_ref[k : k + 1, :], 0.0)
        top, middle, _ = three_terms(s)
        part = dict_ref[:, rows(at, step_f)]
        base[...] += dot(part, top.astype(BF16)) + dot(part, middle.astype(BF16))
        return 0

    lax.fori_loop(0, feats // step_f, steer, 0)

    ri, ci = iota((RC, R), 0), iota((RC, R), 1)
    turn = n_a - lax.rem(y, n_f) * (n_a // n_f) + shift // n_f
    block_no = sum((ri >= B * k).astype(I32) for k in range(1, n_a))
    place_no = (block_no + turn) & (n_a - 1)

    def spot(core):
        return (ci == (place_no * C + core) * B + ri - block_no * B).astype(F32)

    for k in range(C):
        base_c[k] = lax.dot_general(
            base[...], spot(k), NT, preferred_element_type=F32, precision=lax.Precision.HIGHEST
        )

    def attend(q3, mask, rs, first, heads):
        lane = iota((S, HEAD), 1)
        extra = jnp.zeros((S, HEAD), F32)
        for i in range(heads):
            cols = slice((first + i) * HEAD, (first + i + 1) * HEAD)
            mine = slice(i * HEAD, (i + 1) * HEAD)
            s = dot(q3[:, mine], sk_ref[:, cols], NT) * scale
            s = jnp.where(mask, s, NEG)
            m = jnp.max(s, axis=1, keepdims=True)
            e = jnp.where(mask, jnp.exp(s - m), 0.0)
            l = jnp.maximum(jnp.sum(e, axis=1, keepdims=True), 1e-30)
            o = dot(e.astype(BF16), sv_ref[:, cols]) / l
            rs[:, mine] = o.astype(BF16)
            for k, term in enumerate(three_terms(m + jnp.log(l))):
                extra = jnp.where(lane == k * heads + i, term, extra)
        rs[:, heads * HEAD :] = extra.astype(BF16)

    mask_b, mask_a = mask_of(d_b), mask_of(d_a)

    w_step(1)
    e2a.wait()
    lodge = pltpu.make_async_remote_copy(
        src_ref=own_part, dst_ref=part, send_sem=pm_send.at[2], recv_sem=pm_recv.at[2],
        device_id=host, device_id_type=MESH,
    )

    @pl.when(at_home)
    def _():
        part[...] = own_part[...]

    @pl.when(jnp.logical_not(at_home))
    def _():
        lodge.start()

    attend(q3_a, mask_b, rs_a, 0, heads_a)
    e3a.start()
    e2b.wait()
    attend(q3_b, mask_a, rs_b, heads_a, heads_b)
    e3b.start()

    if wring.steps > 1:
        w_step(2)
    e3a.wait()
    r2_a[...] = dot(to_a, r1_a[...]).astype(BF16)
    e4a.start()
    e3b.wait()
    r2_b[...] = dot(to_b, r1_b[...]).astype(BF16)
    e4b.start()
    def merge(e, r3, att, first, heads):
        got = dot(e, r3[...], TN)
        for i in range(heads):
            h = first + i
            mine = slice(i * HEAD, (i + 1) * HEAD)
            extra = heads * HEAD + i
            lse = sum(got[:, extra + k * heads : extra + k * heads + 1] for k in range(3))
            lse1 = sum(
                part[:, at : at + 1].astype(F32)
                for at in (width + k * (heads_a + heads_b) + h for k in range(3))
            )
            m = jnp.maximum(lse1, lse)
            a, b = jnp.exp(lse1 - m), jnp.exp(lse - m)
            total = a * part[:, h * HEAD : (h + 1) * HEAD].astype(F32) + b * got[:, mine]
            att[:, mine] = (total / (a + b)).astype(BF16)

    def block_a(xi, zi):
        return ag_a.at[xi, lax.div(zi, n_f), lax.rem(zi, n_f)]

    def block_b(xi, zi):
        return ag_b.at[xi, lax.div(zi, n_f), lax.rem(zi, n_f)]

    def place(att, block, at):
        return pltpu.make_async_remote_copy(
            src_ref=att, dst_ref=block(x, z),
            send_sem=pm_send.at[at], recv_sem=pm_recv.at[at],
            device_id=y_id(t_guest), device_id_type=MESH,
        )

    def move(att, block, at):
        @pl.when(in_plane)
        def _():
            block(x, z)[...] = att[...]

        @pl.when(jnp.logical_not(in_plane))
        def _():
            place(att, block, at).start()

    def settle(att, block, at):
        @pl.when(jnp.logical_not(in_plane))
        def _():
            place(att, block, at).wait_recv()

    guest_src, _, _ = split_parents(par_ref[pl.ds(d_guest, 1), :])
    f_a, f_b = slots_of(guest_src, d_a), slots_of(guest_src, d_b)
    @pl.when(jnp.logical_not(at_home))
    def _():
        lodge.wait_recv()

    e4a.wait()
    merge(f_a, r3_a, att_a, 0, heads_a)
    move(att_a, block_a, 0)
    e4b.wait()
    merge(f_b, r3_b, att_b, heads_a, heads_b)
    move(att_b, block_b, 1)

    class Spread:
        def __init__(self, along, across):
            self.along, self.across = along, across

        def jobs(self, r):
            def source():
                if r:
                    self.along.wait(r)
                self.along.start(r + 1)
                fresh = [0] if r == 0 else [-r, r][: 1 if 2 * r == self.along.n else 2]
                if r <= self.along.steps:
                    for o in fresh:
                        self.across[o].start(1)

            def pass_on(ring, step):
                ring.wait(step)
                ring.start(step + 1)

            yield source
            for o, ring in self.across.items():
                if 0 < r - abs(o) <= ring.steps:
                    yield functools.partial(pass_on, ring, r - abs(o))

        def drain(self):
            self.along.drain()
            for ring in self.across.values():
                ring.drain()

    def offsets(n):
        return [0] + [o for k in range(1, n // 2 + 1) for o in ([-k, k] if 2 * k < n else [-k])]

    spread_a = Spread(
        Ring(lambda i, part: block_a(x, i), Z, z, z_id, az_send, az_recv),
        {
            o: Ring(
                lambda i, part, o=o: block_a(i, lax.rem(z + o + Z, Z)),
                X, x, x_id, ax_send.at[k], ax_recv.at[k], last_way=k % 2,
            )
            for k, o in enumerate(offsets(Z))
        },
    )
    spread_b = Spread(
        Ring(lambda i, part: block_b(i, z), X, x, x_id, bx_send, bx_recv),
        {
            o: Ring(
                lambda i, part, o=o: block_b(lax.rem(x + o + X, X), i),
                Z, z, z_id, bz_send.at[k], bz_recv.at[k], last_way=1 - k % 2,
            )
            for k, o in enumerate(offsets(X))
        },
    )
    rounds = (X + Z) // 2

    def multiply(xi, first):
        for bit in range(n_f):
            ys = y_of(xi, bit)
            for ag, at, size in ((ag_a, 0, split), (ag_b, split, wide)):
                weights = wbuf[ys, :, :, at : at + size].reshape(C * W, size)
                part = dot(weights, ag[xi, :, bit].reshape(n_a * B, size), NT)
                if first and bit == 0 and at == 0:
                    acc[...] = part
                else:
                    acc[...] += part

    def weights_here():
        for at, index in enumerate(handed):
            to_sibling(index, at, 1 - c).wait_recv()

    for r in range(rounds + 1):
        if r == 0:
            settle(att_a, block_a, 0)
        for job_a, job_b in itertools.zip_longest(spread_a.jobs(r), spread_b.jobs(r)):
            if job_a:
                job_a()
            if r == 0 and job_b:
                settle(att_b, block_b, 1)
            if job_b:
                job_b()
        if r == 0 and wring.steps > 2:
            w_step(3)
        if r == Z // 4 and wring.steps > 3:
            w_step(4)
        if r == Z // 2:
            weights_here()
        if r >= Z // 2:
            k = r - Z // 2
            multiply(lax.rem(x + k, X), k == 0)
            if 0 < 2 * k < X:
                multiply(lax.rem(x + X - k, X), False)

    swap_out = pltpu.make_async_remote_copy(
        src_ref=acc.at[rows((1 - c) * W, W)], dst_ref=sib,
        send_sem=sb_send, recv_sem=sb_recv, device_id=sibling, device_id_type=MESH,
    )
    swap_out.start()
    acc[rows(c * W, W), :] += base_c[c]

    def join(got, n_each, core):
        n = got.shape[0]
        means, squares = got[:, 2 * core : 2 * core + 1, :], got[:, 2 * core + 1 : 2 * core + 2, :]
        mean = jnp.sum(means, axis=0) * (1.0 / n)
        away = means - mean[None]
        square = jnp.sum(squares, axis=0) + n_each * jnp.sum(away * away, axis=0)
        return mean, square

    row_no = iota((8, RC), 0)

    def pack(stats, core):
        mean, square = stats
        return jnp.where(row_no == core * 2, mean, jnp.where(row_no == core * 2 + 1, square, 0.0))

    def stats_of(value):
        mean = jnp.sum(value, axis=0, keepdims=True) * (1.0 / W)
        away = value - mean
        return mean, jnp.sum(away * away, axis=0, keepdims=True)

    mine = pack(stats_of(acc[rows(c * W, W), :]), c)
    swap_out.wait_recv()
    sib[...] += base_c[1 - c]
    st1[...] = mine + pack(stats_of(sib[...]), 1 - c)
    s1 = Share(st1, g1, NX, xc, xc_id, sh_send.at[0], sh_recv.at[0], 1)
    s1.start()
    eye = iota((W, W), 0) == iota((W, W), 1)
    gain = jnp.sum(jnp.where(eye, gain_ref[...], 0.0), axis=1, keepdims=True)
    bias = jnp.sum(jnp.where(eye, bias_ref[...], 0.0), axis=1, keepdims=True)
    s1.wait()
    st2[...] = sum(pack(join(g1[...], float(W), k), k) for k in range(C))
    s2 = Share(st2, g2, Z, z, z_id, sh_send.at[1], sh_recv.at[1], 1)
    s2.start()
    s2.wait()
    def normed(value, core):
        mean, square = joined[core]
        var = square * (1.0 / (W * NX * Z))
        return ((value - mean) * lax.rsqrt(var + 1e-5) * gain + bias).astype(BF16)

    joined = [join(g2[...], float(W * NX), k) for k in range(C)]
    own = acc[rows(c * W, W), :]
    parts = [normed(jnp.where(c == k, own, sib[...]), k) for k in range(C)]
    out_ref[...] = sum(dot(part, spot(k).astype(BF16)) for k, part in enumerate(parts)).astype(BF16)

    for e in exchanges:
        e.drain()
    s1.drain()
    s2.drain()
    for ring in (wring, spread_a, spread_b):
        ring.drain()

    @pl.when(jnp.logical_not(in_plane))
    def _():
        place(att_a, block_a, 0).wait_send()
        place(att_b, block_b, 1).wait_send()

    @pl.when(jnp.logical_not(at_home))
    def _():
        lodge.wait_send()

    for at, index in enumerate(handed):
        to_sibling(index, at, c).wait_send()
    swap_out.wait_send()


def on_device(
    queries, new_kv, prefix_kv, suffix_kv, suffix_len, parents, out_weight, residual,
    steer_dict, steer_ids, steer_strength, norm_gain, norm_bias,
):
    G = lax.axis_size("dp")
    Y = lax.axis_size("tensor")
    NX = X * C
    S = G * CAP
    B, width = queries.shape
    split, heads_a, heads_b = heads_of(width)
    wide = width - split
    T = suffix_kv.shape[1]
    W = out_weight.shape[1]
    R = residual.shape[0]
    RC = R // C
    VM = pltpu.VMEM
    DMA = pltpu.SemaphoreType.DMA
    n_f = Y // X
    args = (
        queries, new_kv, prefix_kv, suffix_kv,
        (parents * PACK + suffix_len).reshape(G, B),
        out_weight.T, residual.T, steer_dict.T, steer_ids.T, steer_strength.T,
        norm_gain[None], norm_bias[None],
    )
    in_hbm = (1, 2, 3, 5, 7)
    big = max(NX, Z)
    scratch = (
        [VM((S, split), BF16)] * 4
        + [VM((S, wide), BF16)] * 4
        + [VM((S, split + HEAD), BF16)] * 4
        + [VM((S, wide + HEAD), BF16)] * 4
        + [
            VM((B, width + HEAD), BF16), VM((B, width + HEAD), BF16), VM(new_kv.shape, BF16), VM(prefix_kv.shape, BF16), VM(suffix_kv.shape, BF16),
            VM((B * T, width), BF16), VM((B * T, width), BF16), VM(steer_dict.T.shape, BF16),
            VM((B, split), BF16), VM((B, wide), BF16),
            VM((X, Z // n_f, n_f, B, split), BF16), VM((X, Z // n_f, n_f, B, wide), BF16),
            VM((Y, C, W, width), BF16),
            VM((W, R), F32), VM((C, W, RC), F32), VM((C * W, RC), F32), VM((W, RC), F32),
            VM((8, RC), F32), VM((8, RC), F32), VM((NX, 8, RC), F32), VM((Z, 8, RC), F32),
        ]
        + [DMA((8, big))] * 2
        + [DMA((2, big))] * 2
        + [DMA((2, Y // 2))] * 2
        + [DMA((Y,))] * 2
        + [DMA((2, Z // 2))] * 2
        + [DMA((Z, 2, X // 2))] * 2
        + [DMA((2, X // 2))] * 2
        + [DMA((X, 2, Z // 2))] * 2
        + [DMA((4,))] * 2
        + [DMA((6,)), DMA, DMA]
    )
    out = pl.pallas_call(
        functools.partial(kernel, Y),
        out_shape=jax.ShapeDtypeStruct((W, R), BF16),
        in_specs=[pl.BlockSpec(memory_space=pl.ANY if i in in_hbm else VM) for i in range(len(args))],
        out_specs=pl.BlockSpec(memory_space=VM),
        scratch_shapes=scratch,
        compiler_params=pltpu.CompilerParams(
            collective_id=0, has_side_effects=True, vmem_limit_bytes=56 * 1024 * 1024
        ),
        name="beam_step",
    )(*args)
    return out.T


def solution(mesh):
    placed = (
        P("dp", "tensor"),
        P("dp", None, "tensor"),
        P(None, None, "tensor"),
        P("dp", None, None, "tensor"),
        P(),
        P(),
        P("tensor", "dp"),
        P("tensor", "dp"),
        P(None, "dp"),
        P("tensor", None),
        P("tensor", None),
        P("dp"),
        P("dp"),
    )
    return jax.shard_map(
        on_device, mesh=mesh, in_specs=placed, out_specs=P("tensor", "dp"), check_vma=False
    )
```
